128 devices in a mesh: dp: 8 (over y, core), tensor: 16 (over x, z).
Axes of the slice: x: 4, y: 4, z: 4, core: 2. Of those that a mesh axis runs over, the one named last changes fastest.
Arguments:
- gradients: bfloat16 [8, 3072, 12288], P('dp', None, 'tensor'), may hold values from -40 to 40
- errors: bfloat16 [8, 3072, 12288], P('dp', None, 'tensor'), may hold values from -2 to 2
- weight: bfloat16 [3072, 12288], P(None, 'tensor'), may hold values from -6 to 6
- start_q: float32 [12288, 64], P('tensor'), may hold values from -6 to 6
Outputs:
- new_errors: bfloat16 [8, 3072, 12288], P('dp', None, 'tensor')
- new_weight: bfloat16 [3072, 12288], P(None, 'tensor')
- right_factor: float32 [12288, 64], P('tensor')
The draws below stay inside these ranges and needn't reach their ends.
All inputs are finite; a program needn't handle non-finite values.
Results may differ from the reference program's by a relative error of at most 0.001.
Values sent between devices are 32-bit elements; how exact they have to be, the bound alone decides.
No kernel may reach another device: no remote copies, remote signals or barrier semaphores. Data moves between devices by JAX's collectives and lax.ppermute only.
A program may use at most 128 MiB of HBM per device.

```python
import math
import jax
import jax.numpy as jnp
from jax import lax

ROWS = 3072
COLS = 12288
RANK = 64
ITERS = 2
REPLICAS = 8


def draw_gradients(key, part):
    key = jax.random.fold_in(key, 7)
    first, second, third = jax.random.split(key, 3)
    row_scale = jnp.exp(jax.random.uniform(first, (ROWS, 1), jnp.float32) * math.log(10.0)) / 3.0
    col_scale = jnp.exp(jax.random.uniform(second, (1, COLS), jnp.float32, math.log(0.5), math.log(2.0)))
    noise = jnp.clip(jax.random.normal(third, (REPLICAS, ROWS, COLS), jnp.float32), -4.0, 4.0)
    rising = (1.0 + 2.0 * jnp.arange(REPLICAS, dtype=jnp.float32) / (REPLICAS - 1)) / 2.0
    base = noise
    return (base * row_scale[None] * col_scale[None] * rising[:, None, None]).astype(jnp.bfloat16)


def steps_of(key, shape, shards, smallest, top_value):
    def one(axis_at, parts):
        heights = jax.random.uniform(jax.random.fold_in(jax.random.fold_in(key, 6), axis_at), (parts,), jnp.float32, smallest / len(shards), top_value / len(shards))
        return jnp.repeat(jnp.exp(heights), shape[axis_at] // parts).reshape((-1,) + (1,) * (len(shape) - axis_at - 1))

    gain = one(*shards[0])
    for cut in shards[1:]:
        gain = gain * one(*cut)
    return gain


def normal_values(key, extent, scale, reach, cuts=(), held_as=jnp.bfloat16):
    values = jax.random.normal(key, extent, jnp.float32) * scale
    if len(cuts) > 0:
        values = steps_of(key, extent, cuts, -0.22, 0.18) * values
    return jnp.clip(values, min=-reach, max=reach).astype(held_as)


def setup_inputs(seed: int = 0) -> dict:
    arg_keys = jax.random.split(jax.random.key(seed), 5)
    return {
        "gradients": draw_gradients(jax.random.fold_in(arg_keys[4], 71), 0),
        "errors": normal_values(arg_keys[1], (REPLICAS, ROWS, COLS), 0.3, 2.0, ((0, 8), (2, 16))),
        "weight": normal_values(arg_keys[2], (ROWS, COLS), 1.0, 6.0, ((1, 16),)),
        "start_q": normal_values(arg_keys[3], (COLS, RANK), 1.0, 6.0, ((0, 16),), jnp.float32),
    }


HIGH = lax.Precision.HIGHEST

def orthonormal(left):
    gram = jnp.dot(left.T.astype(jnp.float32), left.astype(jnp.float32), precision=HIGH, preferred_element_type=jnp.float32)
    chol = jnp.linalg.cholesky(gram)
    return lax.linalg.triangular_solve(chol, left, left_side=False, lower=True, transpose_a=True)

def reference(gradients, errors, weight, start_q):
    right_factor = start_q
    basis = None
    for step in range(ITERS):

        def add_left(total, pair):
            merged = pair[0].astype(jnp.float32) + pair[1].astype(jnp.float32)
            return (total + jnp.dot(merged.astype(jnp.float32), right_factor.astype(jnp.float32), precision=HIGH, preferred_element_type=jnp.float32), None)
        left, unused = lax.scan(add_left, jnp.zeros((ROWS, RANK), jnp.float32), (gradients, errors))
        basis = orthonormal(left / REPLICAS)

        def add_right(total, pair):
            merged = pair[0].astype(jnp.float32) + pair[1].astype(jnp.float32)
            return (total + jnp.dot(merged.T.astype(jnp.float32), basis.astype(jnp.float32), precision=HIGH, preferred_element_type=jnp.float32), None)
        right, unused = lax.scan(add_right, jnp.zeros((COLS, RANK), jnp.float32), (gradients, errors))
        right_factor = right / REPLICAS
    approx = jnp.dot(basis.astype(jnp.float32), right_factor.T.astype(jnp.float32), precision=HIGH, preferred_element_type=jnp.float32)

    def renew(pair):
        merged = pair[0].astype(jnp.float32) + pair[1].astype(jnp.float32)
        return (merged - approx).astype(jnp.bfloat16)
    new_errors = lax.map(renew, (gradients, errors))
    new_weight = (weight.astype(jnp.float32) - 0.5 * approx).astype(jnp.bfloat16)
    return (new_errors, new_weight, right_factor)
```

```python
import functools

import jax
import jax.numpy as jnp
from jax import lax
from jax.experimental import pallas as pl
from jax.experimental.pallas import tpu as pltpu
from jax.sharding import Mesh, PartitionSpec as P

F32, BF16 = jnp.float32, jnp.bfloat16
HIGH = lax.Precision.HIGHEST
RANK, HALF = 64, 32
ROWS, COLS = 3072, 768
BLOCK = 768
BLOCKS = ROWS // BLOCK
CHIPS = 64
REPLICAS = 8
CHIP_AXES = ("y", "x", "z")
LIMIT = 40 * 2**20


def split(x, parts):
    terms = []
    for _ in range(parts):
        term = x.astype(BF16)
        terms.append(term)
        x = x - term.astype(F32)
    return terms


def fold(x):
    return x[:RANK] + (x[RANK : 2 * RANK] + x[2 * RANK :])


def ordered(core, mine, other):
    first = core == 0
    return jnp.concatenate([jnp.where(first, mine, other), jnp.where(first, other, mine)], axis=0)


def parted(core, x):
    first = core == 0
    top, bottom = x[:HALF], x[HALF:]
    return jnp.where(first, top, bottom), jnp.where(first, bottom, top)


def left_kernel(first, core, *refs):
    if first:
        q, g, e, mine, other, stack = refs
    else:
        z_mine, z_other, inverse, g, e, mine, other, stack = refs

    @pl.when(pl.program_id(0) == 0)
    def _():
        if first:
            right = q[...].T
        else:
            z = ordered(core[0], z_mine[...], z_other[...])
            right = jnp.dot(inverse[...], z, precision=HIGH, preferred_element_type=F32) * (1.0 / REPLICAS)
        stack[...] = jnp.concatenate(split(right, 3), axis=0)

    across = (((1,), (1,)), ((), ()))
    p = lax.dot_general(stack[...], g[...], across, preferred_element_type=F32)
    p = p + lax.dot_general(stack[...], e[...], across, preferred_element_type=F32)
    mine[0], other[0] = parted(core[0], fold(p))


def right_kernel(core, l_mine, l_other, g, e, z_mine, z_other, gram, total, products):
    step = pl.program_id(0)

    @pl.when(step == 0)
    def _():
        total[...] = jnp.zeros_like(total)
        products[...] = jnp.zeros_like(products)

    left = ordered(core[0], l_mine[0], l_other[0])
    stack = jnp.concatenate(split(left, 3), axis=0)
    z = jnp.dot(stack, g[...], preferred_element_type=F32)
    total[...] += fold(z + jnp.dot(stack, e[...], preferred_element_type=F32))
    products[...] += lax.dot_general(stack, stack, (((1,), (1,)), ((), ())), preferred_element_type=F32)

    @pl.when(step == BLOCKS - 1)
    def _():
        z_mine[...], z_other[...] = parted(core[0], total[...])
        rows = fold(products[...])
        gram[...] = rows[:, :RANK] + (rows[:, RANK : 2 * RANK] + rows[:, 2 * RANK :])


def factor_kernel(gram, inverse):
    rows = lax.broadcasted_iota(jnp.int32, (RANK, RANK), 0)
    cols = lax.broadcasted_iota(jnp.int32, (RANK, RANK), 1)
    work = jnp.concatenate([gram[...], (rows == cols).astype(F32)], axis=1)
    for k in range(RANK):
        scale = lax.rsqrt(work[k : k + 1, k : k + 1])
        row = work[k : k + 1, :] * scale
        inverse[k : k + 1, :] = row[:, RANK:]
        start = (k + 1) // 8 * 8
        if start >= RANK:
            break
        column = work[start:, k : k + 1] * scale
        below = lax.broadcasted_iota(jnp.int32, (RANK - start, 1), 0) + start > k
        rest = work[start:] - jnp.where(below, column, 0.0) * row
        work = jnp.concatenate([work[:start], rest], axis=0) if start else rest


def renew_kernel(core, z_mine, z_other, inverse, l_mine, l_other, g, e, w, new_e, new_w, right_out, stack):
    @pl.when(pl.program_id(0) == 0)
    def _():
        z = ordered(core[0], z_mine[...], z_other[...])
        right = jnp.dot(inverse[...], z, precision=HIGH, preferred_element_type=F32) * (1.0 / REPLICAS)
        right_out[...] = right.T
        mixed = lax.dot_general(
            inverse[...], right, (((0,), (0,)), ((), ())), precision=HIGH, preferred_element_type=F32
        )
        high, low = split(mixed, 2)
        stack[...] = jnp.concatenate([high, low, high], axis=0)

    left = ordered(core[0], l_mine[0], l_other[0])
    high, low = split(left, 2)
    factors = jnp.concatenate([high, high, low], axis=0)
    approx = lax.dot_general(factors, stack[...], (((0,), (0,)), ((), ())), preferred_element_type=F32)
    merged = g[...].astype(F32) + e[...].astype(F32)
    new_e[...] = (merged - approx).astype(BF16)
    new_w[...] = (w[...].astype(F32) - 0.5 * approx).astype(BF16)


def spec(shape, index):
    return pl.BlockSpec(shape, index)


def whole(shape):
    return pl.BlockSpec(shape, lambda i: (0,) * len(shape))


SCALAR = pl.BlockSpec(memory_space=pltpu.SMEM)
TILE = spec((BLOCK, COLS), lambda i: (i, 0))
PIECE = spec((1, HALF, BLOCK), lambda i: (i, 0, 0))
PIECES = jax.ShapeDtypeStruct((BLOCKS, HALF, BLOCK), F32)
ZHALF = jax.ShapeDtypeStruct((HALF, COLS), F32)


def cost(products, nbytes):
    return pl.CostEstimate(flops=2 * ROWS * COLS * RANK * products, bytes_accessed=nbytes, transcendentals=0)


def params():
    return pltpu.CompilerParams(vmem_limit_bytes=LIMIT, dimension_semantics=("arbitrary",))


def left_pass(core, right, g, e):
    first = len(right) == 1
    if first:
        specs = [whole((COLS, RANK))]
    else:
        specs = [whole((HALF, COLS)), whole((HALF, COLS)), whole((RANK, RANK))]
    return pl.pallas_call(
        functools.partial(left_kernel, first),
        grid=(BLOCKS,),
        in_specs=[SCALAR, *specs, TILE, TILE],
        out_specs=[PIECE, PIECE],
        out_shape=[PIECES, PIECES],
        scratch_shapes=[pltpu.VMEM((3 * RANK, COLS), BF16)],
        compiler_params=params(),
        cost_estimate=cost(6, 4 * ROWS * COLS),
        name="left_pass",
    )(core, *right, g, e)


def right_pass(core, l_mine, l_other, g, e):
    return pl.pallas_call(
        right_kernel,
        grid=(BLOCKS,),
        in_specs=[SCALAR, PIECE, PIECE, TILE, TILE],
        out_specs=[whole((HALF, COLS)), whole((HALF, COLS)), whole((RANK, RANK))],
        out_shape=[ZHALF, ZHALF, jax.ShapeDtypeStruct((RANK, RANK), F32)],
        scratch_shapes=[pltpu.VMEM((RANK, COLS), F32), pltpu.VMEM((3 * RANK, 3 * RANK), F32)],
        compiler_params=params(),
        cost_estimate=cost(6, 4 * ROWS * COLS),
        name="right_pass",
    )(core, l_mine, l_other, g, e)


def factor(gram):
    return pl.pallas_call(
        factor_kernel,
        out_shape=jax.ShapeDtypeStruct((RANK, RANK), F32),
        cost_estimate=pl.CostEstimate(flops=2 * RANK**3, bytes_accessed=8 * RANK**2, transcendentals=RANK),
        name="factor",
    )(gram)


def renew(core, z_mine, z_other, inverse, l_mine, l_other, g, e, w):
    array = jax.ShapeDtypeStruct((ROWS, COLS), BF16)
    return pl.pallas_call(
        renew_kernel,
        grid=(BLOCKS,),
        in_specs=[SCALAR, whole((HALF, COLS)), whole((HALF, COLS)), whole((RANK, RANK)), PIECE, PIECE, TILE, TILE, TILE],
        out_specs=[TILE, TILE, whole((COLS, RANK))],
        out_shape=[array, array, jax.ShapeDtypeStruct((COLS, RANK), F32)],
        scratch_shapes=[pltpu.VMEM((3 * RANK, COLS), BF16)],
        compiler_params=params(),
        cost_estimate=cost(3, 10 * ROWS * COLS),
        name="renew",
    )(core, z_mine, z_other, inverse, l_mine, l_other, g, e, w)


def swap(x):
    return lax.ppermute(x, "core", [(0, 1), (1, 0)])


def along_y(x, shift):
    return lax.ppermute(x, "y", [(i, (i + shift) % 4) for i in range(4)])


def sum_left(mine, other):
    term = (mine + swap(other)).reshape(CHIPS, 2, BLOCK)
    term = lax.all_to_all(term, CHIP_AXES, 0, 0, tiled=True)
    term = jnp.sum(term, axis=0, keepdims=True) * (1.0 / REPLICAS)
    term = jnp.broadcast_to(term, (CHIPS, 2, BLOCK))
    term = lax.all_to_all(term, CHIP_AXES, 0, 0, tiled=True)
    term = term.reshape(BLOCKS, HALF, BLOCK)
    return term, swap(term)


def sum_right(mine, other):
    half = mine + swap(other)
    parts = [along_y(half, shift) for shift in (1, 3, 2)]
    half = half + parts[0] + parts[1] + parts[2]
    return half, swap(half)


def shards(gradients, errors, weight, start_q):
    g, e = gradients[0], errors[0]
    core = lax.axis_index("core").astype(jnp.int32).reshape(1)
    left = sum_left(*left_pass(core, (start_q,), g, e))
    z_mine, z_other, gram = right_pass(core, *left, g, e)
    right = (*sum_right(z_mine, z_other), factor(gram))
    left = sum_left(*left_pass(core, right, g, e))
    z_mine, z_other, gram = right_pass(core, *left, g, e)
    right = (*sum_right(z_mine, z_other), factor(gram))
    new_e, new_w, right_factor = renew(core, *right, *left, g, e, weight)
    return new_e[None], new_w, right_factor


def solution(mesh):
    chips = Mesh(mesh.devices.reshape(4, 2, 4, 4), ("y", "core", "x", "z"))
    dp, tensor = ("y", "core"), ("x", "z")
    return jax.shard_map(
        shards,
        mesh=chips,
        in_specs=(P(dp, None, tensor), P(dp, None, tensor), P(None, tensor), P(tensor, None)),
        out_specs=(P(dp, None, tensor), P(None, tensor), P(tensor, None)),
        check_vma=False,
    )
```

```python
import jax
import jax.numpy as jnp
from jax import lax
from jax.experimental import pallas as pl
from jax.experimental.pallas import tpu as pltpu
from jax.sharding import Mesh, PartitionSpec as P

F32, BF16 = jnp.float32, jnp.bfloat16
HIGH = lax.Precision.HIGHEST
RANK, HALF = 64, 32
ROWS, COLS = 3072, 768
BLOCK = 768
BLOCKS = ROWS // BLOCK
WIDE = 256
SLAB = 384
SLABS = ROWS // SLAB
CHIPS = 64
TILES = HALF * ROWS // 512
REPLICAS = 8
CHIP_AXES = ("y", "x", "z")
LIMIT, SMALL = 32 * 2**20, 8 * 2**20


def split(x, parts):
    terms = []
    for _ in range(parts):
        term = x.astype(BF16)
        terms.append(term)
        x = x - term.astype(F32)
    return terms


def fold(x):
    return x[:RANK] + (x[RANK : 2 * RANK] + x[2 * RANK :])


def ordered(core, mine, other):
    first = core == 0
    return jnp.concatenate([jnp.where(first, mine, other), jnp.where(first, other, mine)], axis=0)


def parted(core, x):
    first = core == 0
    top, bottom = x[:HALF], x[HALF:]
    return jnp.where(first, top, bottom), jnp.where(first, bottom, top)


def put(pieces, block, x):
    for lane in range(BLOCK // 128):
        for group in range(HALF // 4):
            tile = (block * (BLOCK // 128) + lane) * (HALF // 4) + group
            pieces[tile] = x[4 * group : 4 * group + 4, 128 * lane : 128 * lane + 128]


def take(pieces, block):
    columns = []
    for lane in range(BLOCK // 128):
        start = (block * (BLOCK // 128) + lane) * (HALF // 4)
        columns.append(jnp.concatenate([pieces[start + group] for group in range(HALF // 4)], axis=0))
    return jnp.concatenate(columns, axis=1)


def put_both(core, mine, other, block, x):
    for pieces, half in zip((mine, other), parted(core, x)):
        put(pieces, block, half)


def mean_kernel(terms, out):
    share = terms[...].reshape(CHIPS, TILES // CHIPS, 4, 128)
    total = jnp.sum(share, axis=0) * (1.0 / REPLICAS)
    out[...] = jnp.broadcast_to(total[None], share.shape).reshape(out.shape)


def stacked(x):
    return jnp.concatenate(split(x, 3), axis=0)


def times_rows(stack, g, e, block):
    rows = pl.ds(block * BLOCK, BLOCK)
    across = (((1,), (1,)), ((), ()))
    p = lax.dot_general(stack[...], g[rows, :], across, preferred_element_type=F32)
    return fold(p + lax.dot_general(stack[...], e[rows, :], across, preferred_element_type=F32))


def first_left_kernel(core, q, g_far, e_far, mine, other, g, e, stack, g_sem, e_sem):
    copies = []
    for block in range(BLOCKS):
        rows = pl.ds(block * BLOCK, BLOCK)
        pair = (
            pltpu.make_async_copy(g_far.at[rows, :], g.at[rows, :], g_sem.at[block]),
            pltpu.make_async_copy(e_far.at[rows, :], e.at[rows, :], e_sem.at[block]),
        )
        for copy in pair:
            copy.start()
        copies.append(pair)
    stack[...] = stacked(q[...])
    for block, pair in enumerate(copies):
        for copy in pair:
            copy.wait()
        put_both(core[0], mine, other, block, times_rows(stack, g, e, block))


def left_kernel(core, z_mine, z_other, inverse, g, e, mine, other, stack):
    z = ordered(core[0], z_mine[...], z_other[...])
    right = jnp.dot(inverse[...], z, precision=HIGH, preferred_element_type=F32) * (1.0 / REPLICAS)
    stack[...] = stacked(right)
    for block in range(BLOCKS):
        put_both(core[0], mine, other, block, times_rows(stack, g, e, block))


def right_kernel(core, l_mine, l_other, g, e, z_mine, z_other, gram, stack):
    for block in range(BLOCKS):
        left = ordered(core[0], take(l_mine, block), take(l_other, block))
        stack[:, pl.ds(block * BLOCK, BLOCK)] = stacked(left)
    for part in range(COLS // WIDE):
        cols = pl.ds(part * WIDE, WIDE)
        z = jnp.dot(stack[...], g[:, cols], preferred_element_type=F32)
        z = fold(z + jnp.dot(stack[...], e[:, cols], preferred_element_type=F32))
        z_mine[:, cols], z_other[:, cols] = parted(core[0], z)
    products = lax.dot_general(stack[...], stack[...], (((1,), (1,)), ((), ())), preferred_element_type=F32)
    rows = fold(products)
    gram[...] = rows[:, :RANK] + (rows[:, RANK : 2 * RANK] + rows[:, 2 * RANK :])


def factor_kernel(gram, inverse):
    rows = lax.broadcasted_iota(jnp.int32, (RANK, RANK), 0)
    cols = lax.broadcasted_iota(jnp.int32, (RANK, RANK), 1)
    work = jnp.concatenate([gram[...], (rows == cols).astype(F32)], axis=1)
    for start in range(0, RANK, 8):
        column = [jnp.broadcast_to(work[:, start + j : start + j + 1], work.shape) for j in range(8)]
        row = [work[j : j + 1, :] for j in range(8)]
        for j in range(8):
            pivot = column[j][j : j + 1, :]
            inverse[start + j : start + j + 1, :] = (row[j] * lax.rsqrt(pivot))[:, RANK:]
            scaled = row[j] / pivot
            for i in range(j + 1, 8):
                factor = column[i][j : j + 1, :] / pivot
                row[i] = row[i] - column[i][j : j + 1, :] * scaled
                column[i] = column[i] - column[j] * factor
            if start + 8 < RANK:
                work = work - column[j] * scaled
        work = work[8:]


def renew_kernel(
    core, z_mine, z_other, inverse, l_mine, l_other, g, e, w_far, new_e, new_w, right_out, stack, e_near, w_near, in_sem, e_sem, w_sem
):
    def rows(step):
        return pl.ds(step * SLAB, SLAB)

    loads = []
    for step in range(SLABS):
        loads.append(pltpu.make_async_copy(w_far.at[rows(step), :], w_near.at[rows(step), :], in_sem.at[step]))
        loads[-1].start()
    z = ordered(core[0], z_mine[...], z_other[...])
    right = jnp.dot(inverse[...], z, precision=HIGH, preferred_element_type=F32) * (1.0 / REPLICAS)
    right_out[...] = right
    mixed = lax.dot_general(inverse[...], right, (((0,), (0,)), ((), ())), precision=HIGH, preferred_element_type=F32)
    high, low = split(mixed, 2)
    stack[...] = jnp.concatenate([high, low, high], axis=0)
    stores = []
    for step in range(SLABS):
        block, within = divmod(step * SLAB, BLOCK)
        if within == 0:
            whole = ordered(core[0], take(l_mine, block), take(l_other, block))
        left = whole[:, within : within + SLAB]
        high, low = split(left, 2)
        factors = jnp.concatenate([high, high, low], axis=0)
        approx = lax.dot_general(factors, stack[...], (((0,), (0,)), ((), ())), preferred_element_type=F32)
        merged = g[rows(step), :].astype(F32) + e[rows(step), :].astype(F32)
        e_near[rows(step), :] = (merged - approx).astype(BF16)
        stores.append(pltpu.make_async_copy(e_near.at[rows(step), :], new_e.at[rows(step), :], e_sem.at[step]))
        stores[-1].start()
        loads[step].wait()
        w_near[rows(step), :] = (w_near[rows(step), :].astype(F32) - 0.5 * approx).astype(BF16)
        stores.append(pltpu.make_async_copy(w_near.at[rows(step), :], new_w.at[rows(step), :], w_sem.at[step]))
        stores[-1].start()
    for store in stores:
        store.wait()


SCALAR = pl.BlockSpec(memory_space=pltpu.SMEM)
NEAR = pl.BlockSpec(memory_space=pltpu.VMEM)
FAR = pl.BlockSpec(memory_space=pltpu.HBM)
PIECES = jax.ShapeDtypeStruct((TILES, 4, 128), F32)
ZHALF = jax.ShapeDtypeStruct((HALF, COLS), F32)
SQUARE = jax.ShapeDtypeStruct((RANK, RANK), F32)
STACK = pltpu.VMEM((3 * RANK, COLS), BF16)


def cost(products, nbytes):
    return pl.CostEstimate(flops=2 * ROWS * COLS * RANK * products, bytes_accessed=nbytes, transcendentals=0)


def params(limit):
    return pltpu.CompilerParams(vmem_limit_bytes=limit)


def near(*arrays):
    return [pltpu.with_memory_space_constraint(x, pltpu.VMEM) for x in arrays]


def far(*arrays):
    return [pltpu.with_memory_space_constraint(x, pltpu.HBM) for x in arrays]


def first_left_pass(core, q, g, e):
    return pl.pallas_call(
        first_left_kernel,
        in_specs=[SCALAR, NEAR, FAR, FAR],
        out_specs=[NEAR] * 4,
        out_shape=[PIECES, PIECES, pltpu.VMEM((ROWS, COLS), BF16), pltpu.VMEM((ROWS, COLS), BF16)],
        scratch_shapes=[STACK, pltpu.SemaphoreType.DMA((BLOCKS,)), pltpu.SemaphoreType.DMA((BLOCKS,))],
        compiler_params=params(LIMIT),
        cost_estimate=cost(6, 4 * ROWS * COLS),
        name="first_left_pass",
    )(core, q, *far(g, e))


def left_pass(core, z_mine, z_other, inverse, g, e):
    return pl.pallas_call(
        left_kernel,
        in_specs=[SCALAR] + [NEAR] * 5,
        out_specs=[NEAR] * 2,
        out_shape=[PIECES, PIECES],
        scratch_shapes=[STACK],
        compiler_params=params(LIMIT),
        cost_estimate=cost(6, 4 * ROWS * COLS),
        name="left_pass",
    )(core, z_mine, z_other, inverse, *near(g, e))


def right_pass(core, l_mine, l_other, g, e):
    return pl.pallas_call(
        right_kernel,
        in_specs=[SCALAR] + [NEAR] * 4,
        out_specs=[NEAR] * 3,
        out_shape=[ZHALF, ZHALF, SQUARE],
        scratch_shapes=[pltpu.VMEM((3 * RANK, ROWS), BF16)],
        compiler_params=params(LIMIT),
        cost_estimate=cost(6, 4 * ROWS * COLS),
        name="right_pass",
    )(core, l_mine, l_other, *near(g, e))


def factor(gram):
    return pl.pallas_call(
        factor_kernel,
        out_shape=SQUARE,
        compiler_params=params(SMALL),
        cost_estimate=pl.CostEstimate(flops=4 * 10**9, bytes_accessed=8 * RANK**2, transcendentals=RANK),
        name="factor",
    )(gram)


def renew(core, z_mine, z_other, inverse, l_mine, l_other, g, e, w):
    array = jax.ShapeDtypeStruct((ROWS, COLS), BF16)
    return pl.pallas_call(
        renew_kernel,
        in_specs=[SCALAR] + [NEAR] * 7 + [FAR],
        out_specs=[FAR, FAR, NEAR],
        out_shape=[array, array, jax.ShapeDtypeStruct((RANK, COLS), F32)],
        scratch_shapes=[
            STACK,
            pltpu.VMEM((ROWS, COLS), BF16),
            pltpu.VMEM((ROWS, COLS), BF16),
            *[pltpu.SemaphoreType.DMA((SLABS,)) for _ in range(3)],
        ],
        compiler_params=params(LIMIT),
        cost_estimate=cost(3, 10 * ROWS * COLS),
        name="renew",
    )(core, z_mine, z_other, inverse, l_mine, l_other, *near(g, e), *far(w))


def swap(x):
    return lax.ppermute(x, "core", [(0, 1), (1, 0)])


def along_y(x, shift):
    return lax.ppermute(x, "y", [(i, (i + shift) % 4) for i in range(4)])


def mean(terms):
    return pl.pallas_call(
        mean_kernel,
        out_shape=PIECES,
        compiler_params=params(SMALL),
        cost_estimate=pl.CostEstimate(flops=HALF * ROWS, bytes_accessed=8 * HALF * ROWS, transcendentals=0),
        name="mean",
    )(terms)


def exchange(x):
    x = x.reshape(CHIPS, TILES // CHIPS, 4, 128)
    return lax.all_to_all(x, CHIP_AXES, 0, 0, tiled=True).reshape(TILES, 4, 128)


def sum_left(mine, other):
    term = exchange(mean(exchange(mine + swap(other))))
    return term, swap(term)


def sum_right(mine, other):
    half = mine + swap(other)
    parts = [along_y(half, shift) for shift in (1, 3, 2)]
    half = half + parts[0] + parts[1] + parts[2]
    return half, swap(half)


def shards(gradients, errors, weight, start_q):
    g, e = gradients[0], errors[0]
    core = lax.axis_index("core").astype(jnp.int32).reshape(1)
    mine, other, g, e = first_left_pass(core, start_q.T, g, e)
    left = sum_left(mine, other)
    z_mine, z_other, gram = right_pass(core, *left, g, e)
    right = (*sum_right(z_mine, z_other), factor(gram))
    left = sum_left(*left_pass(core, *right, g, e))
    z_mine, z_other, gram = right_pass(core, *left, g, e)
    right = (*sum_right(z_mine, z_other), factor(gram))
    new_e, new_w, right_factor = renew(core, *right, *left, g, e, weight)
    return new_e[None], new_w, right_factor.T


def solution(mesh):
    chips = Mesh(mesh.devices.reshape(4, 2, 4, 4), ("y", "core", "x", "z"))
    dp, tensor = ("y", "core"), ("x", "z")
    return jax.shard_map(
        shards,
        mesh=chips,
        in_specs=(P(dp, None, tensor), P(dp, None, tensor), P(None, tensor), P(tensor, None)),
        out_specs=(P(dp, None, tensor), P(None, tensor), P(tensor, None)),
        check_vma=False,
    )
```

```python
import jax
import jax.numpy as jnp
from jax import lax
from jax.experimental import pallas as pl
from jax.experimental.pallas import tpu as pltpu
from jax.sharding import Mesh, PartitionSpec as P

F32, BF16 = jnp.float32, jnp.bfloat16
HIGH = lax.Precision.HIGHEST
RANK, HALF = 64, 32
ROWS, COLS = 3072, 768
WIDE = 256
EVEN = (1024,) * 3
LAST = (256,) * 12
CHIPS = 64
TILES = HALF * ROWS // 512
REPLICAS = 8
CHIP_AXES = ("y", "x", "z")
LIMIT, SMALL = 32 * 2**20, 8 * 2**20


def split(x, parts):
    terms = []
    for _ in range(parts):
        term = x.astype(BF16)
        terms.append(term)
        x = x - term.astype(F32)
    return terms


def fold(x):
    return x[:RANK] + (x[RANK : 2 * RANK] + x[2 * RANK :])


def ordered(core, mine, other):
    first = core == 0
    return jnp.concatenate([jnp.where(first, mine, other), jnp.where(first, other, mine)], axis=0)


def parted(core, x):
    first = core == 0
    top, bottom = x[:HALF], x[HALF:]
    return jnp.where(first, top, bottom), jnp.where(first, bottom, top)


def put(pieces, start, x):
    for lane in range(x.shape[1] // 128):
        for group in range(HALF // 4):
            tile = (start // 128 + lane) * (HALF // 4) + group
            pieces[tile] = x[4 * group : 4 * group + 4, 128 * lane : 128 * lane + 128]


def take(pieces, start, size):
    columns = []
    for lane in range(start // 128, (start + size) // 128):
        tiles = [pieces[lane * (HALF // 4) + group] for group in range(HALF // 4)]
        columns.append(jnp.concatenate(tiles, axis=0))
    return jnp.concatenate(columns, axis=1)


def put_both(core, mine, other, start, x):
    for pieces, half in zip((mine, other), parted(core, x)):
        put(pieces, start, half)


def take_both(core, mine, other, start, size):
    return ordered(core, take(mine, start, size), take(other, start, size))


def ranges(sizes):
    starts = [sum(sizes[:i]) for i in range(len(sizes))]
    return list(zip(starts, sizes))


def mean_kernel(terms, out):
    share = terms[...].reshape(CHIPS, TILES // CHIPS, 4, 128)
    total = jnp.sum(share, axis=0) * (1.0 / REPLICAS)
    out[...] = jnp.broadcast_to(total[None], share.shape).reshape(out.shape)


def stacked(x):
    return jnp.concatenate(split(x, 3), axis=0)


def times_rows(stack, g, e, start, size):
    rows = pl.ds(start, size)
    across = (((1,), (1,)), ((), ()))
    p = lax.dot_general(stack[...], g[rows, :], across, preferred_element_type=F32)
    return fold(p + lax.dot_general(stack[...], e[rows, :], across, preferred_element_type=F32))


def first_left_kernel(core, q_far, g_far, e_far, mine, other, g, e, stack, q, q_sem, g_sem, e_sem):
    q_copy = pltpu.make_async_copy(q_far, q, q_sem)
    q_copy.start()
    pieces = ranges(EVEN)
    copies = []
    for i, (start, size) in enumerate(pieces):
        rows = pl.ds(start, size)
        copies.append(
            (
                pltpu.make_async_copy(g_far.at[rows, :], g.at[rows, :], g_sem.at[i]),
                pltpu.make_async_copy(e_far.at[rows, :], e.at[rows, :], e_sem.at[i]),
            )
        )
    for pair in copies[:2]:
        for copy in pair:
            copy.start()
    q_copy.wait()
    stack[...] = stacked(q[...])
    for i, (start, size) in enumerate(pieces):
        for copy in copies[i]:
            copy.wait()
        for copy in copies[i + 2] if i + 2 < len(copies) else ():
            copy.start()
        put_both(core[0], mine, other, start, times_rows(stack, g, e, start, size))


def left_kernel(core, z_mine, z_other, inverse, g, e, mine, other, stack):
    z = ordered(core[0], z_mine[...], z_other[...])
    right = jnp.dot(inverse[...], z, precision=HIGH, preferred_element_type=F32) * (1.0 / REPLICAS)
    stack[...] = stacked(right)
    for start, size in ranges(EVEN):
        put_both(core[0], mine, other, start, times_rows(stack, g, e, start, size))


def right_kernel(core, l_mine, l_other, g, e, z_mine, z_other, gram, stack):
    for start, size in ranges(EVEN):
        stack[:, pl.ds(start, size)] = stacked(take_both(core[0], l_mine, l_other, start, size))
    for part in range(COLS // WIDE):
        cols = pl.ds(part * WIDE, WIDE)
        z = jnp.dot(stack[...], g[:, cols], preferred_element_type=F32)
        z = fold(z + jnp.dot(stack[...], e[:, cols], preferred_element_type=F32))
        z_mine[:, cols], z_other[:, cols] = parted(core[0], z)
    products = lax.dot_general(stack[...], stack[...], (((1,), (1,)), ((), ())), preferred_element_type=F32)
    rows = fold(products)
    gram[...] = rows[:, :RANK] + (rows[:, RANK : 2 * RANK] + rows[:, 2 * RANK :])


def factor_kernel(gram, inverse):
    rows = lax.broadcasted_iota(jnp.int32, (RANK, RANK), 0)
    cols = lax.broadcasted_iota(jnp.int32, (RANK, RANK), 1)
    work = jnp.concatenate([gram[...], (rows == cols).astype(F32)], axis=1)
    for start in range(0, RANK, 8):
        column = [jnp.broadcast_to(work[:, start + j : start + j + 1], work.shape) for j in range(8)]
        row = [work[j : j + 1, :] for j in range(8)]
        for j in range(8):
            pivot = column[j][j : j + 1, :]
            inverse[start + j : start + j + 1, :] = (row[j] * lax.rsqrt(pivot))[:, RANK:]
            scaled = row[j] / pivot
            for i in range(j + 1, 8):
                factor = column[i][j : j + 1, :] / pivot
                row[i] = row[i] - column[i][j : j + 1, :] * scaled
                column[i] = column[i] - column[j] * factor
            if start + 8 < RANK:
                work = work - column[j] * scaled
        work = work[8:]


def ready_kernel(core, l_mine, l_other, w_far, factors, w, w_sem):
    load = pltpu.make_async_copy(w_far, w, w_sem)
    load.start()
    for start, size in ranges(EVEN):
        high, low = split(take_both(core[0], l_mine, l_other, start, size), 2)
        factors[pl.ds(start, size), :] = jnp.concatenate([high, high, low], axis=0).T
    load.wait()


def renew_kernel(core, z_mine, z_other, inverse, factors, g, e, w, new_e, new_w, right_out, e_near, w_near, e_sem, w_sem):
    z = ordered(core[0], z_mine[...], z_other[...])
    right = jnp.dot(inverse[...], z, precision=HIGH, preferred_element_type=F32) * (1.0 / REPLICAS)
    right_out[...] = right
    mixed = lax.dot_general(inverse[...], right, (((0,), (0,)), ((), ())), precision=HIGH, preferred_element_type=F32)
    high, low = split(mixed, 2)
    stack = jnp.concatenate([high, low, high], axis=0)
    stores = []
    for i, (start, size) in enumerate(ranges(LAST)):
        rows = pl.ds(start, size)
        approx = jnp.dot(factors[rows, :], stack, preferred_element_type=F32)
        merged = g[rows, :].astype(F32) + e[rows, :].astype(F32)
        e_near[rows, :] = (merged - approx).astype(BF16)
        stores.append(pltpu.make_async_copy(e_near.at[rows, :], new_e.at[rows, :], e_sem.at[i]))
        stores[-1].start()
        w_near[rows, :] = (w[rows, :].astype(F32) - 0.5 * approx).astype(BF16)
        stores.append(pltpu.make_async_copy(w_near.at[rows, :], new_w.at[rows, :], w_sem.at[i]))
        stores[-1].start()
    for store in stores:
        store.wait()


SCALAR = pl.BlockSpec(memory_space=pltpu.SMEM)
NEAR = pl.BlockSpec(memory_space=pltpu.VMEM)
FAR = pl.BlockSpec(memory_space=pltpu.HBM)
PIECES = jax.ShapeDtypeStruct((TILES, 4, 128), F32)
ZHALF = jax.ShapeDtypeStruct((HALF, COLS), F32)
NEAR_ARRAY = pltpu.VMEM((ROWS, COLS), BF16)
SQUARE = jax.ShapeDtypeStruct((RANK, RANK), F32)
STACK = pltpu.VMEM((3 * RANK, COLS), BF16)


def cost(products, nbytes):
    return pl.CostEstimate(flops=2 * ROWS * COLS * RANK * products, bytes_accessed=nbytes, transcendentals=0)


def params(limit):
    return pltpu.CompilerParams(vmem_limit_bytes=limit)


def near(*arrays):
    return [pltpu.with_memory_space_constraint(x, pltpu.VMEM) for x in arrays]


def far(*arrays):
    return [pltpu.with_memory_space_constraint(x, pltpu.HBM) for x in arrays]


def semaphores(count):
    return pltpu.SemaphoreType.DMA((count,))


def first_left_pass(core, q, g, e):
    return pl.pallas_call(
        first_left_kernel,
        in_specs=[SCALAR, FAR, FAR, FAR],
        out_specs=[NEAR] * 4,
        out_shape=[PIECES, PIECES, NEAR_ARRAY, NEAR_ARRAY],
        scratch_shapes=[
            STACK,
            pltpu.VMEM((RANK, COLS), F32),
            pltpu.SemaphoreType.DMA,
            semaphores(len(EVEN)),
            semaphores(len(EVEN)),
        ],
        compiler_params=params(LIMIT),
        cost_estimate=cost(6, 4 * ROWS * COLS),
        name="first_left_pass",
    )(core, *far(q, g, e))


def left_pass(core, z_mine, z_other, inverse, g, e):
    return pl.pallas_call(
        left_kernel,
        in_specs=[SCALAR] + [NEAR] * 5,
        out_specs=[NEAR] * 2,
        out_shape=[PIECES, PIECES],
        scratch_shapes=[STACK],
        compiler_params=params(LIMIT),
        cost_estimate=cost(6, 4 * ROWS * COLS),
        name="left_pass",
    )(core, z_mine, z_other, inverse, *near(g, e))


def right_pass(core, l_mine, l_other, g, e):
    return pl.pallas_call(
        right_kernel,
        in_specs=[SCALAR] + [NEAR] * 4,
        out_specs=[NEAR] * 3,
        out_shape=[ZHALF, ZHALF, SQUARE],
        scratch_shapes=[pltpu.VMEM((3 * RANK, ROWS), BF16)],
        compiler_params=params(LIMIT),
        cost_estimate=cost(6, 4 * ROWS * COLS),
        name="right_pass",
    )(core, l_mine, l_other, *near(g, e))


def factor(gram):
    return pl.pallas_call(
        factor_kernel,
        out_shape=SQUARE,
        compiler_params=params(SMALL),
        cost_estimate=pl.CostEstimate(flops=4 * 10**9, bytes_accessed=8 * RANK**2, transcendentals=RANK),
        name="factor",
    )(gram)


def ready(core, l_mine, l_other, w):
    return pl.pallas_call(
        ready_kernel,
        in_specs=[SCALAR, NEAR, NEAR, FAR],
        out_specs=[NEAR] * 2,
        out_shape=[pltpu.VMEM((ROWS, 3 * RANK), BF16), NEAR_ARRAY],
        scratch_shapes=[pltpu.SemaphoreType.DMA],
        compiler_params=params(SMALL),
        cost_estimate=cost(1, 4 * ROWS * COLS),
        name="ready",
    )(core, l_mine, l_other, *far(w))


def renew(core, z_mine, z_other, inverse, factors, g, e, w):
    array = jax.ShapeDtypeStruct((ROWS, COLS), BF16)
    return pl.pallas_call(
        renew_kernel,
        in_specs=[SCALAR] + [NEAR] * 7,
        out_specs=[FAR, FAR, NEAR],
        out_shape=[array, array, jax.ShapeDtypeStruct((RANK, COLS), F32)],
        scratch_shapes=[
            pltpu.VMEM((ROWS, COLS), BF16),
            pltpu.VMEM((ROWS, COLS), BF16),
            semaphores(len(LAST)),
            semaphores(len(LAST)),
        ],
        compiler_params=params(LIMIT),
        cost_estimate=cost(3, 10 * ROWS * COLS),
        name="renew",
    )(core, z_mine, z_other, inverse, *near(factors, g, e, w))


def swap(x):
    return lax.ppermute(x, "core", [(0, 1), (1, 0)])


def along_y(x, shift):
    return lax.ppermute(x, "y", [(i, (i + shift) % 4) for i in range(4)])


def mean(terms):
    return pl.pallas_call(
        mean_kernel,
        out_shape=PIECES,
        compiler_params=params(SMALL),
        cost_estimate=pl.CostEstimate(flops=HALF * ROWS, bytes_accessed=8 * HALF * ROWS, transcendentals=0),
        name="mean",
    )(terms)


def exchange(x):
    x = x.reshape(CHIPS, TILES // CHIPS, 4, 128)
    return lax.all_to_all(x, CHIP_AXES, 0, 0, tiled=True).reshape(TILES, 4, 128)


def sum_left(mine, other):
    term = exchange(mean(exchange(mine + swap(other))))
    return term, swap(term)


def sum_right(mine, other, beside=None):
    half = mine + swap(other)
    if beside is not None:
        step, args = beside
        half, args = lax.optimization_barrier((half, args))
        done = step(*args)
    parts = [along_y(half, shift) for shift in (1, 3, 2)]
    if beside is not None:
        parts, done = lax.optimization_barrier((parts, done))
    half = half + parts[0] + parts[1] + parts[2]
    both = (half, swap(half))
    return both if beside is None else (both, done)


def shards(gradients, errors, weight, start_q):
    core = lax.axis_index("core").astype(jnp.int32).reshape(1)
    mine, other, g, e = first_left_pass(core, start_q.T, gradients[0], errors[0])
    left = sum_left(mine, other)
    z_mine, z_other, gram = right_pass(core, *left, g, e)
    right = sum_right(z_mine, z_other)
    left = sum_left(*left_pass(core, *right, factor(gram), g, e))
    z_mine, z_other, gram = right_pass(core, *left, g, e)
    right, (factors, w) = sum_right(z_mine, z_other, (ready, (core, *left, weight)))
    new_e, new_w, right_factor = renew(core, *right, factor(gram), factors, g, e, w)
    return new_e[None], new_w, right_factor.T


def solution(mesh):
    chips = Mesh(mesh.devices.reshape(4, 2, 4, 4), ("y", "core", "x", "z"))
    dp, tensor = ("y", "core"), ("x", "z")
    return jax.shard_map(
        shards,
        mesh=chips,
        in_specs=(P(dp, None, tensor), P(dp, None, tensor), P(None, tensor), P(tensor, None)),
        out_specs=(P(dp, None, tensor), P(None, tensor), P(tensor, None)),
        check_vma=False,
    )
```

```python
import jax
import jax.numpy as jnp
from jax import lax
from jax.experimental import pallas as pl
from jax.experimental.pallas import tpu as pltpu
from jax.sharding import Mesh, PartitionSpec as P

F32, BF16 = jnp.float32, jnp.bfloat16
HIGH = lax.Precision.HIGHEST
RANK, HALF = 64, 32
ROWS, COLS = 3072, 768
WIDE = 256
OWN = ROWS // 2
EVEN = (1024,) * 3
PART = (768,) * 2
LAST = (256,) * 12
CHIPS = 64
TILES = HALF * ROWS // 512
REPLICAS = 8
CHIP_AXES = ("y", "x", "z")
LIMIT, SMALL = 16 * 2**20, 6 * 2**20


def split(x, parts):
    terms = []
    for _ in range(parts):
        term = x.astype(BF16)
        terms.append(term)
        x = x - term.astype(F32)
    return terms


def fold(x):
    return x[:RANK] + (x[RANK : 2 * RANK] + x[2 * RANK :])


def ordered(core, mine, other):
    first = core == 0
    return jnp.concatenate([jnp.where(first, mine, other), jnp.where(first, other, mine)], axis=0)


def parted(core, x):
    first = core == 0
    top, bottom = x[:HALF], x[HALF:]
    return jnp.where(first, top, bottom), jnp.where(first, bottom, top)


def put(pieces, start, x):
    groups = x.shape[0] // 4
    for lane in range(x.shape[1] // 128):
        for group in range(groups):
            tile = (start // 128 + lane) * groups + group
            pieces[tile] = x[4 * group : 4 * group + 4, 128 * lane : 128 * lane + 128]


def take(pieces, start, size):
    groups = RANK // 4
    columns = []
    for lane in range(start // 128, (start + size) // 128):
        tiles = [pieces[lane * groups + group] for group in range(groups)]
        columns.append(jnp.concatenate(tiles, axis=0))
    return jnp.concatenate(columns, axis=1)


def put_rows(core, mine, other, start, x):
    for half in range(2):
        low, high = max(start, half * OWN), min(start + x.shape[1], (half + 1) * OWN)
        if low < high:
            own = x[:, low - start : high - start]

            @pl.when(core == half)
            def _():
                put(mine, low - half * OWN, own)

            @pl.when(core != half)
            def _():
                put(other, low - half * OWN, own)


def ranges(sizes):
    starts = [sum(sizes[:i]) for i in range(len(sizes))]
    return list(zip(starts, sizes))


def mean_kernel(terms, out):
    share = terms[...].reshape(CHIPS, TILES // CHIPS, 4, 128)
    total = jnp.sum(share, axis=0) * (1.0 / REPLICAS)
    out[...] = jnp.broadcast_to(total[None], share.shape).reshape(out.shape)


def stacked(x):
    return jnp.concatenate(split(x, 3), axis=0)


def times_rows(stack, g, e, start, size):
    rows = pl.ds(start, size)
    across = (((1,), (1,)), ((), ()))
    p = lax.dot_general(stack[...], g[rows, :], across, preferred_element_type=F32)
    return fold(p + lax.dot_general(stack[...], e[rows, :], across, preferred_element_type=F32))


def first_left_kernel(core, q_far, g_far, e_far, mine, other, g, e, stack, q, q_sem, g_sem, e_sem):
    q_copy = pltpu.make_async_copy(q_far, q, q_sem)
    q_copy.start()
    pieces = ranges(EVEN)
    copies = []
    for i, (start, size) in enumerate(pieces):
        rows = pl.ds(start, size)
        copies.append(
            (
                pltpu.make_async_copy(g_far.at[rows, :], g.at[rows, :], g_sem.at[i]),
                pltpu.make_async_copy(e_far.at[rows, :], e.at[rows, :], e_sem.at[i]),
            )
        )
    for pair in copies[:2]:
        for copy in pair:
            copy.start()
    q_copy.wait()
    stack[...] = stacked(q[...])
    for i, (start, size) in enumerate(pieces):
        for copy in copies[i]:
            copy.wait()
        for copy in copies[i + 2] if i + 2 < len(copies) else ():
            copy.start()
        put_rows(core[0], mine, other, start, times_rows(stack, g, e, start, size))


def right_stack(core, z_mine, z_other, inverse):
    z = ordered(core[0], z_mine[...], z_other[...])
    return stacked(jnp.dot(inverse[...], z, precision=HIGH, preferred_element_type=F32) * (1.0 / REPLICAS))


def give_kernel(core, g, e, send):
    for start in range(0, OWN, 256):
        rows = pl.ds(pl.multiple_of((1 - core[0]) * OWN + start, 256), 256)
        send[pl.ds(start, 256), :] = g[rows, :].astype(F32) + e[rows, :].astype(F32)


def merge_kernel(core, g, e, received, high, low):
    for start in range(0, OWN, 256):
        rows = pl.ds(pl.multiple_of(core[0] * OWN + start, 256), 256)
        here = pl.ds(start, 256)
        total = g[rows, :].astype(F32) + e[rows, :].astype(F32) + received[here, :]
        high[here, :], low[here, :] = split(total, 2)


def left_kernel(core, z_mine, z_other, inverse, high, low, term, stack):
    stack[...] = right_stack(core, z_mine, z_other, inverse)
    for start, size in ranges(PART):
        put(term, start, times_rows(stack, high, low, start, size))


def right_kernel(core, left, high, low, z_mine, z_other, gram, stack):
    for start, size in ranges(PART):
        stack[:, pl.ds(start, size)] = stacked(take(left, start, size))
    for part in range(COLS // WIDE):
        cols = pl.ds(part * WIDE, WIDE)
        z = jnp.dot(stack[...], high[:, cols], preferred_element_type=F32)
        z = fold(z + jnp.dot(stack[...], low[:, cols], preferred_element_type=F32))
        z_mine[:, cols], z_other[:, cols] = parted(core[0], z)
    products = lax.dot_general(stack[...], stack[...], (((1,), (1,)), ((), ())), preferred_element_type=F32)
    rows = fold(products)
    gram[...] = rows[:, :RANK] + (rows[:, RANK : 2 * RANK] + rows[:, 2 * RANK :])


def factor_kernel(grams, inverse):
    rows = lax.broadcasted_iota(jnp.int32, (RANK, RANK), 0)
    cols = lax.broadcasted_iota(jnp.int32, (RANK, RANK), 1)
    gram = sum(part[...] for part in grams)
    work = jnp.concatenate([gram, (rows == cols).astype(F32)], axis=1)
    for start in range(0, RANK, 8):
        column = [jnp.broadcast_to(work[:, start + j : start + j + 1], work.shape) for j in range(8)]
        row = [work[j : j + 1, :] for j in range(8)]
        for j in range(8):
            pivot = column[j][j : j + 1, :]
            inverse[start + j : start + j + 1, :] = (row[j] * lax.rsqrt(pivot))[:, RANK:]
            scaled = row[j] / pivot
            for i in range(j + 1, 8):
                factor = column[i][j : j + 1, :] / pivot
                row[i] = row[i] - column[i][j : j + 1, :] * scaled
                column[i] = column[i] - column[j] * factor
            if start + 8 < RANK:
                work = work - column[j] * scaled
        work = work[8:]


def ready_kernel(core, l_mine, l_other, w_far, factors, w, w_sem):
    load = pltpu.make_async_copy(w_far, w, w_sem)
    load.start()
    for pieces, base in ((l_mine, core[0]), (l_other, 1 - core[0])):
        for start, size in ranges(PART):
            high, low = split(take(pieces, start, size), 2)
            rows = pl.ds(pl.multiple_of(base * OWN + start, 256), size)
            factors[rows, :] = jnp.concatenate([high, high, low], axis=0).T
    load.wait()


def renew_kernel(core, z_mine, z_other, inverse, factors, g, e, w, new_e, new_w, right_out, e_near, w_near, e_sem, w_sem):
    z = ordered(core[0], z_mine[...], z_other[...])
    right = jnp.dot(inverse[...], z, precision=HIGH, preferred_element_type=F32) * (1.0 / REPLICAS)
    right_out[...] = right
    mixed = lax.dot_general(inverse[...], right, (((0,), (0,)), ((), ())), precision=HIGH, preferred_element_type=F32)
    high, low = split(mixed, 2)
    stack = jnp.concatenate([high, low, high], axis=0)
    stores = []
    for i, (start, size) in enumerate(ranges(LAST)):
        rows = pl.ds(start, size)
        approx = jnp.dot(factors[rows, :], stack, preferred_element_type=F32)
        merged = g[rows, :].astype(F32) + e[rows, :].astype(F32)
        e_near[rows, :] = (merged - approx).astype(BF16)
        stores.append(pltpu.make_async_copy(e_near.at[rows, :], new_e.at[rows, :], e_sem.at[i]))
        stores[-1].start()
        w_near[rows, :] = (w[rows, :].astype(F32) - 0.5 * approx).astype(BF16)
        stores.append(pltpu.make_async_copy(w_near.at[rows, :], new_w.at[rows, :], w_sem.at[i]))
        stores[-1].start()
    for store in stores:
        store.wait()


SCALAR = pl.BlockSpec(memory_space=pltpu.SMEM)
NEAR = pl.BlockSpec(memory_space=pltpu.VMEM)
FAR = pl.BlockSpec(memory_space=pltpu.HBM)
PIECES = jax.ShapeDtypeStruct((TILES, 4, 128), F32)
ZHALF = jax.ShapeDtypeStruct((HALF, COLS), F32)
NEAR_ARRAY = pltpu.VMEM((ROWS, COLS), BF16)
NEAR_HALF = pltpu.VMEM((OWN, COLS), BF16)
SQUARE = jax.ShapeDtypeStruct((RANK, RANK), F32)
STACK = pltpu.VMEM((3 * RANK, COLS), BF16)


def cost(products, nbytes):
    return pl.CostEstimate(flops=2 * ROWS * COLS * RANK * products, bytes_accessed=nbytes, transcendentals=0)


def params(limit):
    return pltpu.CompilerParams(vmem_limit_bytes=limit)


def near(*arrays):
    return [pltpu.with_memory_space_constraint(x, pltpu.VMEM) for x in arrays]


def far(*arrays):
    return [pltpu.with_memory_space_constraint(x, pltpu.HBM) for x in arrays]


def semaphores(count):
    return pltpu.SemaphoreType.DMA((count,))


def first_left_pass(core, q, g, e):
    return pl.pallas_call(
        first_left_kernel,
        in_specs=[SCALAR, FAR, FAR, FAR],
        out_specs=[NEAR] * 4,
        out_shape=[PIECES, PIECES, NEAR_ARRAY, NEAR_ARRAY],
        scratch_shapes=[
            STACK,
            pltpu.VMEM((RANK, COLS), F32),
            pltpu.SemaphoreType.DMA,
            semaphores(len(EVEN)),
            semaphores(len(EVEN)),
        ],
        compiler_params=params(LIMIT),
        cost_estimate=cost(6, 4 * ROWS * COLS),
        name="first_left_pass",
    )(core, *far(q, g, e))


def give(core, g, e):
    return pl.pallas_call(
        give_kernel,
        in_specs=[SCALAR] + [NEAR] * 2,
        out_specs=NEAR,
        out_shape=pltpu.VMEM((OWN, COLS), F32),
        compiler_params=params(SMALL),
        cost_estimate=pl.CostEstimate(flops=10**9, bytes_accessed=8 * OWN * COLS, transcendentals=0),
        name="give",
    )(core, *near(g, e))


def merge(core, g, e, received):
    return pl.pallas_call(
        merge_kernel,
        in_specs=[SCALAR] + [NEAR] * 3,
        out_specs=[NEAR] * 2,
        out_shape=[NEAR_HALF, NEAR_HALF],
        compiler_params=params(SMALL),
        cost_estimate=pl.CostEstimate(flops=10**9, bytes_accessed=8 * OWN * COLS, transcendentals=0),
        name="merge",
    )(core, *near(g, e, received))


def left_pass(core, z_mine, z_other, inverse, high, low):
    return pl.pallas_call(
        left_kernel,
        in_specs=[SCALAR] + [NEAR] * 5,
        out_specs=NEAR,
        out_shape=PIECES,
        scratch_shapes=[STACK],
        compiler_params=params(SMALL),
        cost_estimate=cost(3, 2 * ROWS * COLS),
        name="left_pass",
    )(core, z_mine, z_other, inverse, *near(high, low))


def right_pass(core, left, high, low):
    return pl.pallas_call(
        right_kernel,
        in_specs=[SCALAR] + [NEAR] * 3,
        out_specs=[NEAR] * 3,
        out_shape=[ZHALF, ZHALF, SQUARE],
        scratch_shapes=[pltpu.VMEM((3 * RANK, OWN), BF16)],
        compiler_params=params(SMALL),
        cost_estimate=cost(3, 2 * ROWS * COLS),
        name="right_pass",
    )(core, left, *near(high, low))


def factor(*grams):
    return pl.pallas_call(
        factor_kernel,
        out_shape=SQUARE,
        compiler_params=params(SMALL),
        cost_estimate=pl.CostEstimate(flops=4 * 10**9, bytes_accessed=8 * RANK**2, transcendentals=RANK),
        name="factor",
    )(grams)


def ready(core, l_mine, l_other, w):
    return pl.pallas_call(
        ready_kernel,
        in_specs=[SCALAR, NEAR, NEAR, FAR],
        out_specs=[NEAR] * 2,
        out_shape=[pltpu.VMEM((ROWS, 3 * RANK), BF16), NEAR_ARRAY],
        scratch_shapes=[pltpu.SemaphoreType.DMA],
        compiler_params=params(SMALL),
        cost_estimate=cost(1, 4 * ROWS * COLS),
        name="ready",
    )(core, l_mine, l_other, *far(w))


def renew(core, z_mine, z_other, inverse, factors, g, e, w):
    array = jax.ShapeDtypeStruct((ROWS, COLS), BF16)
    return pl.pallas_call(
        renew_kernel,
        in_specs=[SCALAR] + [NEAR] * 7,
        out_specs=[FAR, FAR, NEAR],
        out_shape=[array, array, jax.ShapeDtypeStruct((RANK, COLS), F32)],
        scratch_shapes=[
            pltpu.VMEM((ROWS, COLS), BF16),
            pltpu.VMEM((ROWS, COLS), BF16),
            semaphores(len(LAST)),
            semaphores(len(LAST)),
        ],
        compiler_params=params(LIMIT),
        cost_estimate=cost(3, 10 * ROWS * COLS),
        name="renew",
    )(core, z_mine, z_other, inverse, *near(factors, g, e, w))


def swap(x):
    return lax.ppermute(x, "core", [(0, 1), (1, 0)])


def along_y(x, shift):
    return lax.ppermute(x, "y", [(i, (i + shift) % 4) for i in range(4)])


def mean(terms):
    return pl.pallas_call(
        mean_kernel,
        out_shape=PIECES,
        compiler_params=params(SMALL),
        cost_estimate=pl.CostEstimate(flops=HALF * ROWS, bytes_accessed=8 * HALF * ROWS, transcendentals=0),
        name="mean",
    )(terms)


def exchange(x):
    x = x.reshape(CHIPS, TILES // CHIPS, 4, 128)
    return lax.all_to_all(x, CHIP_AXES, 0, 0, tiled=True).reshape(TILES, 4, 128)


def mean_left(term):
    return exchange(mean(exchange(term)))


def sum_right(mine, other, run=None):
    half, given = lax.optimization_barrier((mine + swap(other), run[1] if run else ()))
    parts = [along_y(half, shift) for shift in (1, 3, 2)]
    parts, done = lax.optimization_barrier((parts, run[0](*given) if run else ()))
    half = half + parts[0] + parts[1] + parts[2]
    return (half, swap(half)), done


def shards(gradients, errors, weight, start_q):
    core = lax.axis_index("core").astype(jnp.int32).reshape(1)
    mine, other, g, e = first_left_pass(core, start_q.T, gradients[0], errors[0])
    term, send = lax.optimization_barrier((mine + swap(other), give(core, g, e)))
    left, received = lax.optimization_barrier((mean_left(term), swap(send)))
    high, low = merge(core, g, e, received)
    z_mine, z_other, gram = right_pass(core, left, high, low)
    right, _ = sum_right(z_mine, z_other)
    left = mean_left(left_pass(core, *right, factor(gram, swap(gram)), high, low))
    left_other = swap(left)
    z_mine, z_other, gram = right_pass(core, left, high, low)
    right, (factors, w) = sum_right(z_mine, z_other, (ready, (core, left, left_other, weight)))
    new_e, new_w, right_factor = renew(core, *right, factor(gram, swap(gram)), factors, g, e, w)
    return new_e[None], new_w, right_factor.T


def solution(mesh):
    chips = Mesh(mesh.devices.reshape(4, 2, 4, 4), ("y", "core", "x", "z"))
    dp, tensor = ("y", "core"), ("x", "z")
    return jax.shard_map(
        shards,
        mesh=chips,
        in_specs=(P(dp, None, tensor), P(dp, None, tensor), P(None, tensor), P(tensor, None)),
        out_specs=(P(dp, None, tensor), P(None, tensor), P(tensor, None)),
        check_vma=False,
    )
```

```python
import jax
import jax.numpy as jnp
from jax import lax
from jax.experimental import pallas as pl
from jax.experimental.pallas import tpu as pltpu
from jax.sharding import Mesh, PartitionSpec as P

F32, BF16 = jnp.float32, jnp.bfloat16
RANK, HALF = 64, 32
ROWS, COLS = 3072, 768
WIDE = 256
OWN = ROWS // 2
EVEN = (1024,) * 3
PART = (512,) * 3
LAST = (256,) * 12
CHIPS = 64
TILES = HALF * ROWS // 512
REPLICAS = 8
CHIP_AXES = ("y", "x", "z")
LIMIT, SMALL = 16 * 2**20, 6 * 2**20


def split(x, parts):
    terms = []
    for _ in range(parts):
        term = x.astype(BF16)
        terms.append(term)
        x = x - term.astype(F32)
    return terms


def fold(x):
    return x[:RANK] + (x[RANK : 2 * RANK] + x[2 * RANK :])


def ordered(core, mine, other):
    first = core == 0
    return jnp.concatenate([jnp.where(first, mine, other), jnp.where(first, other, mine)], axis=0)


def parted(core, x):
    first = core == 0
    top, bottom = x[:HALF], x[HALF:]
    return jnp.where(first, top, bottom), jnp.where(first, bottom, top)


def put(pieces, start, x):
    groups = x.shape[0] // 4
    for lane in range(x.shape[1] // 128):
        for group in range(groups):
            tile = (start // 128 + lane) * groups + group
            pieces[tile] = x[4 * group : 4 * group + 4, 128 * lane : 128 * lane + 128]


def take(pieces, start, size):
    groups = RANK // 4
    columns = []
    for lane in range(start // 128, (start + size) // 128):
        tiles = [pieces[lane * groups + group] for group in range(groups)]
        columns.append(jnp.concatenate(tiles, axis=0))
    return jnp.concatenate(columns, axis=1)


def put_rows(core, mine, other, start, x):
    for half in range(2):
        low, high = max(start, half * OWN), min(start + x.shape[1], (half + 1) * OWN)
        if low < high:
            own = x[:, low - start : high - start]

            @pl.when(core == half)
            def _():
                put(mine, low - half * OWN, own)

            @pl.when(core != half)
            def _():
                put(other, low - half * OWN, own)


def ranges(sizes):
    starts = [sum(sizes[:i]) for i in range(len(sizes))]
    return list(zip(starts, sizes))


def mean_kernel(terms, out):
    share = terms[...].reshape(CHIPS, TILES // CHIPS, 4, 128)
    total = jnp.sum(share, axis=0) * (1.0 / REPLICAS)
    out[...] = jnp.broadcast_to(total[None], share.shape).reshape(out.shape)


def stacked(x):
    return jnp.concatenate(split(x, 3), axis=0)


def times_rows(stack, g, e, start, size):
    rows = pl.ds(start, size)
    across = (((1,), (1,)), ((), ()))
    p = lax.dot_general(stack[...], g[rows, :], across, preferred_element_type=F32)
    return fold(p + lax.dot_general(stack[...], e[rows, :], across, preferred_element_type=F32))


def first_left_kernel(core, q_far, g_far, e_far, mine, other, g, e, stack, q, q_sem, g_sem, e_sem):
    q_copy = pltpu.make_async_copy(q_far, q, q_sem)
    q_copy.start()
    pieces = ranges(EVEN)
    copies = []
    for i, (start, size) in enumerate(pieces):
        rows = pl.ds(start, size)
        copies.append(
            (
                pltpu.make_async_copy(g_far.at[rows, :], g.at[rows, :], g_sem.at[i]),
                pltpu.make_async_copy(e_far.at[rows, :], e.at[rows, :], e_sem.at[i]),
            )
        )
    for pair in copies[:2]:
        for copy in pair:
            copy.start()
    q_copy.wait()
    stack[...] = stacked(q[...])
    for i, (start, size) in enumerate(pieces):
        for copy in copies[i]:
            copy.wait()
        for copy in copies[i + 2] if i + 2 < len(copies) else ():
            copy.start()
        put_rows(core[0], mine, other, start, times_rows(stack, g, e, start, size))


def right_factor(core, z_mine, z_other, inverse):
    z = ordered(core[0], z_mine[...], z_other[...])
    return product(inverse[...], z) * (1.0 / REPLICAS)


def give_kernel(core, g, e, send):
    for start in range(0, OWN, 256):
        rows = pl.ds(pl.multiple_of((1 - core[0]) * OWN + start, 256), 256)
        send[pl.ds(start, 256), :] = g[rows, :].astype(F32) + e[rows, :].astype(F32)


def merge_rows(core, g, e, received, high, low, cols):
    for start in range(0, OWN, 256):
        rows = pl.ds(pl.multiple_of(core[0] * OWN + start, 256), 256)
        here = pl.ds(start, 256)
        total = g[rows, cols].astype(F32) + e[rows, cols].astype(F32) + received[here, cols]
        high[here, cols], low[here, cols] = split(total, 2)


def product(a, b):
    left, right = split(a, 3), split(b, 3)
    pairs = ((0, 2), (1, 1), (2, 0), (0, 1), (1, 0), (0, 0))
    left = jnp.concatenate([left[i] for i, _ in pairs], axis=1)
    right = jnp.concatenate([right[j] for _, j in pairs], axis=0)
    return jnp.dot(left, right, preferred_element_type=F32)


def left_kernel(core, z_mine, z_other, inverse, high, low, term, stack):
    stack[...] = stacked(right_factor(core, z_mine, z_other, inverse))
    for start, size in ranges(PART):
        put(term, start, times_rows(stack, high, low, start, size))


def times_columns(core, stack, first, second, z_mine, z_other, cols):
    z = jnp.dot(stack[...], first[:, cols], preferred_element_type=F32)
    z = fold(z + jnp.dot(stack[...], second[:, cols], preferred_element_type=F32))
    z_mine[:, cols], z_other[:, cols] = parted(core[0], z)


def stack_left(left, stack, gram):
    for start, size in ranges(PART):
        stack[:, pl.ds(start, size)] = stacked(take(left, start, size))
    products = lax.dot_general(stack[...], stack[...], (((1,), (1,)), ((), ())), preferred_element_type=F32)
    rows = fold(products)
    gram[...] = rows[:, :RANK] + (rows[:, RANK : 2 * RANK] + rows[:, 2 * RANK :])


def first_right_kernel(core, left, g, e, received, high, low, z_mine, z_other, gram, stack):
    stack_left(left, stack, gram)
    for part in range(COLS // WIDE):
        cols = pl.ds(part * WIDE, WIDE)
        merge_rows(core, g, e, received, high, low, cols)
        times_columns(core, stack, high, low, z_mine, z_other, cols)


def right_kernel(core, left, high, low, z_mine, z_other, gram, stack):
    stack_left(left, stack, gram)
    for part in range(COLS // WIDE):
        times_columns(core, stack, high, low, z_mine, z_other, pl.ds(part * WIDE, WIDE))


def factor_kernel(grams, inverse):
    rows = lax.broadcasted_iota(jnp.int32, (RANK, RANK), 0)
    cols = lax.broadcasted_iota(jnp.int32, (RANK, RANK), 1)
    gram = sum(part[...] for part in grams)
    work = jnp.concatenate([gram, (rows == cols).astype(F32)], axis=1)
    for start in range(0, RANK, 8):
        column = [jnp.broadcast_to(work[:, start + j : start + j + 1], work.shape) for j in range(8)]
        row = [work[j : j + 1, :] for j in range(8)]
        for j in range(8):
            pivot = column[j][j : j + 1, :]
            inverse[start + j : start + j + 1, :] = (row[j] * lax.rsqrt(pivot))[:, RANK:]
            scaled = row[j] / pivot
            for i in range(j + 1, 8):
                factor = column[i][j : j + 1, :] / pivot
                row[i] = row[i] - column[i][j : j + 1, :] * scaled
                column[i] = column[i] - column[j] * factor
            if start + 8 < RANK:
                work = work - column[j] * scaled
        work = work[8:]


def ready_kernel(core, l_mine, l_other, w_far, factors, w, w_sem):
    load = pltpu.make_async_copy(w_far, w, w_sem)
    load.start()
    for pieces, base in ((l_mine, core[0]), (l_other, 1 - core[0])):
        for start, size in ranges(PART):
            high, low = split(take(pieces, start, size), 2)
            rows = pl.ds(pl.multiple_of(base * OWN + start, 256), size)
            factors[rows, :] = jnp.concatenate([high, high, low], axis=0).T
    load.wait()


def renew_kernel(core, z_mine, z_other, inverse, factors, g, e, w, new_e, new_w, right_out, e_near, w_near, e_sem, w_sem):
    right = right_factor(core, z_mine, z_other, inverse)
    right_out[...] = right
    mixed = product(inverse[...].T, right)
    high, low = split(mixed, 2)
    stack = jnp.concatenate([high, low, high], axis=0)
    stores = []
    for i, (start, size) in enumerate(ranges(LAST)):
        rows = pl.ds(start, size)
        approx = jnp.dot(factors[rows, :], stack, preferred_element_type=F32)
        merged = g[rows, :].astype(F32) + e[rows, :].astype(F32)
        e_near[rows, :] = (merged - approx).astype(BF16)
        stores.append(pltpu.make_async_copy(e_near.at[rows, :], new_e.at[rows, :], e_sem.at[i]))
        stores[-1].start()
        w_near[rows, :] = (w[rows, :].astype(F32) - 0.5 * approx).astype(BF16)
        stores.append(pltpu.make_async_copy(w_near.at[rows, :], new_w.at[rows, :], w_sem.at[i]))
        stores[-1].start()
    for store in stores:
        store.wait()


SCALAR = pl.BlockSpec(memory_space=pltpu.SMEM)
NEAR = pl.BlockSpec(memory_space=pltpu.VMEM)
FAR = pl.BlockSpec(memory_space=pltpu.HBM)
PIECES = jax.ShapeDtypeStruct((TILES, 4, 128), F32)
ZHALF = jax.ShapeDtypeStruct((HALF, COLS), F32)
NEAR_ARRAY = pltpu.VMEM((ROWS, COLS), BF16)
NEAR_HALF = pltpu.VMEM((OWN, COLS), BF16)
SQUARE = jax.ShapeDtypeStruct((RANK, RANK), F32)
STACK = pltpu.VMEM((3 * RANK, COLS), BF16)


def cost(products, nbytes):
    return pl.CostEstimate(flops=2 * ROWS * COLS * RANK * products, bytes_accessed=nbytes, transcendentals=0)


def params(limit):
    return pltpu.CompilerParams(vmem_limit_bytes=limit)


def near(*arrays):
    return [pltpu.with_memory_space_constraint(x, pltpu.VMEM) for x in arrays]


def far(*arrays):
    return [pltpu.with_memory_space_constraint(x, pltpu.HBM) for x in arrays]


def semaphores(count):
    return pltpu.SemaphoreType.DMA((count,))


def first_left_pass(core, q, g, e):
    return pl.pallas_call(
        first_left_kernel,
        in_specs=[SCALAR, FAR, FAR, FAR],
        out_specs=[NEAR] * 4,
        out_shape=[PIECES, PIECES, NEAR_ARRAY, NEAR_ARRAY],
        scratch_shapes=[
            STACK,
            pltpu.VMEM((RANK, COLS), F32),
            pltpu.SemaphoreType.DMA,
            semaphores(len(EVEN)),
            semaphores(len(EVEN)),
        ],
        compiler_params=params(LIMIT),
        cost_estimate=cost(6, 4 * ROWS * COLS),
        name="first_left_pass",
    )(core, *far(q, g, e))


def give(core, g, e):
    return pl.pallas_call(
        give_kernel,
        in_specs=[SCALAR] + [NEAR] * 2,
        out_specs=NEAR,
        out_shape=pltpu.VMEM((OWN, COLS), F32),
        compiler_params=params(SMALL),
        cost_estimate=pl.CostEstimate(flops=10**9, bytes_accessed=8 * OWN * COLS, transcendentals=0),
        name="give",
    )(core, *near(g, e))


def first_right_pass(core, left, g, e, received):
    return pl.pallas_call(
        first_right_kernel,
        in_specs=[SCALAR] + [NEAR] * 4,
        out_specs=[NEAR] * 5,
        out_shape=[NEAR_HALF, NEAR_HALF, ZHALF, ZHALF, SQUARE],
        scratch_shapes=[pltpu.VMEM((3 * RANK, OWN), BF16)],
        compiler_params=params(LIMIT),
        cost_estimate=cost(3, 4 * ROWS * COLS),
        name="first_right_pass",
    )(core, left, *near(g, e, received))


def left_pass(core, z_mine, z_other, inverse, high, low):
    return pl.pallas_call(
        left_kernel,
        in_specs=[SCALAR] + [NEAR] * 5,
        out_specs=NEAR,
        out_shape=PIECES,
        scratch_shapes=[STACK],
        compiler_params=params(SMALL),
        cost_estimate=cost(3, 2 * ROWS * COLS),
        name="left_pass",
    )(core, z_mine, z_other, inverse, *near(high, low))


def right_pass(core, left, high, low):
    return pl.pallas_call(
        right_kernel,
        in_specs=[SCALAR] + [NEAR] * 3,
        out_specs=[NEAR] * 3,
        out_shape=[ZHALF, ZHALF, SQUARE],
        scratch_shapes=[pltpu.VMEM((3 * RANK, OWN), BF16)],
        compiler_params=params(SMALL),
        cost_estimate=cost(3, 2 * ROWS * COLS),
        name="right_pass",
    )(core, left, *near(high, low))


def factor(*grams):
    return pl.pallas_call(
        factor_kernel,
        out_shape=SQUARE,
        compiler_params=params(SMALL),
        cost_estimate=pl.CostEstimate(flops=4 * 10**9, bytes_accessed=8 * RANK**2, transcendentals=RANK),
        name="factor",
    )(grams)


def ready(core, l_mine, l_other, w):
    return pl.pallas_call(
        ready_kernel,
        in_specs=[SCALAR, NEAR, NEAR, FAR],
        out_specs=[NEAR] * 2,
        out_shape=[pltpu.VMEM((ROWS, 3 * RANK), BF16), NEAR_ARRAY],
        scratch_shapes=[pltpu.SemaphoreType.DMA],
        compiler_params=params(SMALL),
        cost_estimate=cost(1, 4 * ROWS * COLS),
        name="ready",
    )(core, l_mine, l_other, *far(w))


def renew(core, z_mine, z_other, inverse, factors, g, e, w):
    array = jax.ShapeDtypeStruct((ROWS, COLS), BF16)
    return pl.pallas_call(
        renew_kernel,
        in_specs=[SCALAR] + [NEAR] * 7,
        out_specs=[FAR, FAR, NEAR],
        out_shape=[array, array, jax.ShapeDtypeStruct((RANK, COLS), F32)],
        scratch_shapes=[
            pltpu.VMEM((ROWS, COLS), BF16),
            pltpu.VMEM((ROWS, COLS), BF16),
            semaphores(len(LAST)),
            semaphores(len(LAST)),
        ],
        compiler_params=params(LIMIT),
        cost_estimate=cost(3, 10 * ROWS * COLS),
        name="renew",
    )(core, z_mine, z_other, inverse, *near(factors, g, e, w))


def swap(x):
    return lax.ppermute(x, "core", [(0, 1), (1, 0)])


def along_y(x, shift):
    return lax.ppermute(x, "y", [(i, (i + shift) % 4) for i in range(4)])


def mean(terms):
    return pl.pallas_call(
        mean_kernel,
        out_shape=PIECES,
        compiler_params=params(SMALL),
        cost_estimate=pl.CostEstimate(flops=HALF * ROWS, bytes_accessed=8 * HALF * ROWS, transcendentals=0),
        name="mean",
    )(terms)


def exchange(x):
    x = x.reshape(CHIPS, TILES // CHIPS, 4, 128)
    return lax.all_to_all(x, CHIP_AXES, 0, 0, tiled=True).reshape(TILES, 4, 128)


def mean_left(term):
    return exchange(mean(exchange(term)))


def sum_right(mine, other, gram, run=None):
    half, grams, given = lax.optimization_barrier((mine + swap(other), (gram, swap(gram)), run[1] if run else ()))
    parts = [along_y(half, shift) for shift in (1, 3, 2)]
    parts, inverse, done = lax.optimization_barrier((parts, factor(*grams), run[0](*given) if run else ()))
    half = (half + parts[2]) + (parts[0] + parts[1])
    return (half, swap(half), inverse), done


def shards(gradients, errors, weight, start_q):
    core = lax.axis_index("core").astype(jnp.int32).reshape(1)
    mine, other, g, e = first_left_pass(core, start_q.T, gradients[0], errors[0])
    term, send = lax.optimization_barrier((mine + swap(other), give(core, g, e)))
    left, received = lax.optimization_barrier((mean_left(term), swap(send)))
    high, low, *terms = first_right_pass(core, left, g, e, received)
    right, _ = sum_right(*terms)
    left = mean_left(left_pass(core, *right, high, low))
    left_other = swap(left)
    right, (factors, w) = sum_right(*right_pass(core, left, high, low), (ready, (core, left, left_other, weight)))
    new_e, new_w, right_factor = renew(core, *right, factors, g, e, w)
    return new_e[None], new_w, right_factor.T


def solution(mesh):
    chips = Mesh(mesh.devices.reshape(4, 2, 4, 4), ("y", "core", "x", "z"))
    dp, tensor = ("y", "core"), ("x", "z")
    return jax.shard_map(
        shards,
        mesh=chips,
        in_specs=(P(dp, None, tensor), P(dp, None, tensor), P(None, tensor), P(tensor, None)),
        out_specs=(P(dp, None, tensor), P(None, tensor), P(tensor, None)),
        check_vma=False,
    )
```

```python
import jax
import jax.numpy as jnp
from jax import lax
from jax.experimental import pallas as pl
from jax.experimental.pallas import tpu as pltpu
from jax.sharding import Mesh, PartitionSpec as P

F32, BF16 = jnp.float32, jnp.bfloat16
RANK, HALF = 64, 32
ROWS, COLS = 3072, 768
WIDE = 256
OWN = ROWS // 2
LOAD = (768,) * 2
PART = (512,) * 3
LAST = (256,) * 12
CHIPS = 64
TILES = HALF * ROWS // 512
REPLICAS = 8
CHIP_AXES = ("y", "x", "z")
LIMIT, SMALL = 16 * 2**20, 6 * 2**20


def split(x, parts):
    terms = []
    for _ in range(parts):
        term = x.astype(BF16)
        terms.append(term)
        x = x - term.astype(F32)
    return terms


def fold(x):
    return x[:RANK] + (x[RANK : 2 * RANK] + x[2 * RANK :])


def ordered(core, mine, other):
    first = core == 0
    return jnp.concatenate([jnp.where(first, mine, other), jnp.where(first, other, mine)], axis=0)


def parted(core, x):
    first = core == 0
    top, bottom = x[:HALF], x[HALF:]
    return jnp.where(first, top, bottom), jnp.where(first, bottom, top)


def put(pieces, start, x):
    groups = x.shape[0] // 4
    for lane in range(x.shape[1] // 128):
        for group in range(groups):
            tile = (start // 128 + lane) * groups + group
            pieces[tile] = x[4 * group : 4 * group + 4, 128 * lane : 128 * lane + 128]


def take(pieces, start, size):
    groups = RANK // 4
    columns = []
    for lane in range(start // 128, (start + size) // 128):
        tiles = [pieces[lane * groups + group] for group in range(groups)]
        columns.append(jnp.concatenate(tiles, axis=0))
    return jnp.concatenate(columns, axis=1)


def ranges(sizes):
    starts = [sum(sizes[:i]) for i in range(len(sizes))]
    return list(zip(starts, sizes))


def mean_kernel(terms, out):
    share = terms[...].reshape(CHIPS, TILES // CHIPS, 4, 128)
    total = jnp.sum(share, axis=0) * (1.0 / REPLICAS)
    out[...] = jnp.broadcast_to(total[None], share.shape).reshape(out.shape)


def stacked(x):
    return jnp.concatenate(split(x, 3), axis=0)


def times_rows(stack, g, e, start, size):
    rows = pl.ds(start, size)
    across = (((1,), (1,)), ((), ()))
    p = lax.dot_general(stack[...], g[rows, :], across, preferred_element_type=F32)
    return fold(p + lax.dot_general(stack[...], e[rows, :], across, preferred_element_type=F32))


def first_other_kernel(core, q_far, g_far, e_far, term, send, g, e, stack, q, q_sem, g_sem, e_sem):
    q_copy = pltpu.make_async_copy(q_far, q, q_sem)
    q_copy.start()
    pieces = ranges(LOAD)
    copies = []
    for half in (1 - core[0], core[0]):
        for start, size in pieces:
            rows = pl.ds(pl.multiple_of(half * OWN + start, 256), size)
            slot = len(copies)
            copies.append(
                (
                    pltpu.make_async_copy(g_far.at[rows, :], g.at[rows, :], g_sem.at[slot]),
                    pltpu.make_async_copy(e_far.at[rows, :], e.at[rows, :], e_sem.at[slot]),
                )
            )
    for pair in copies[: len(pieces)]:
        for copy in pair:
            copy.start()
    q_copy.wait()
    stack[...] = stacked(q[...])
    for pair, later in zip(copies, copies[len(pieces) :]):
        for copy in pair:
            copy.wait()
        for copy in later:
            copy.start()
    for start, size in pieces:
        put(term, start, times_rows(stack, g, e, pl.multiple_of((1 - core[0]) * OWN + start, 256), size))
    for start in range(0, OWN, 256):
        rows = pl.ds(pl.multiple_of((1 - core[0]) * OWN + start, 256), 256)
        send[pl.ds(start, 256), :] = g[rows, :].astype(F32) + e[rows, :].astype(F32)
    for pair in copies[len(pieces) :]:
        for copy in pair:
            copy.wait()


def first_own_kernel(core, stack, g, e, term):
    for half in range(2):

        @pl.when(core[0] == half)
        def _():
            for start, size in ranges(PART):
                put(term, start, times_rows(stack, g, e, half * OWN + start, size))


def right_factor(core, z_mine, z_other, inverse):
    z = ordered(core[0], z_mine[...], z_other[...])
    return product(inverse[...], z) * (1.0 / REPLICAS)


def merge_rows(core, g, e, received, high, low, cols):
    for start in range(0, OWN, 256):
        rows = pl.ds(pl.multiple_of(core[0] * OWN + start, 256), 256)
        here = pl.ds(start, 256)
        total = g[rows, cols].astype(F32) + e[rows, cols].astype(F32) + received[here, cols]
        high[here, cols], low[here, cols] = split(total, 2)


def product(a, b):
    left, right = split(a, 3), split(b, 3)
    pairs = ((0, 2), (1, 1), (2, 0), (0, 1), (1, 0), (0, 0))
    left = jnp.concatenate([left[i] for i, _ in pairs], axis=1)
    right = jnp.concatenate([right[j] for _, j in pairs], axis=0)
    return jnp.dot(left, right, preferred_element_type=F32)


def left_kernel(core, z_mine, z_other, inverse, high, low, term, stack):
    stack[...] = stacked(right_factor(core, z_mine, z_other, inverse))
    for start, size in ranges(PART):
        put(term, start, times_rows(stack, high, low, start, size))


def times_columns(core, stack, first, second, z_mine, z_other, cols):
    z = jnp.dot(stack[...], first[:, cols], preferred_element_type=F32)
    z = fold(z + jnp.dot(stack[...], second[:, cols], preferred_element_type=F32))
    z_mine[:, cols], z_other[:, cols] = parted(core[0], z)


def stack_left(left, stack, gram):
    for start, size in ranges(PART):
        stack[:, pl.ds(start, size)] = stacked(take(left, start, size))
    products = lax.dot_general(stack[...], stack[...], (((1,), (1,)), ((), ())), preferred_element_type=F32)
    rows = fold(products)
    gram[...] = rows[:, :RANK] + (rows[:, RANK : 2 * RANK] + rows[:, 2 * RANK :])


def first_right_kernel(core, left, g, e, received, high, low, z_mine, z_other, gram, stack):
    stack_left(left, stack, gram)
    for part in range(COLS // WIDE):
        cols = pl.ds(part * WIDE, WIDE)
        merge_rows(core, g, e, received, high, low, cols)
        times_columns(core, stack, high, low, z_mine, z_other, cols)


def right_kernel(core, left, high, low, z_mine, z_other, gram, stack):
    stack_left(left, stack, gram)
    for part in range(COLS // WIDE):
        times_columns(core, stack, high, low, z_mine, z_other, pl.ds(part * WIDE, WIDE))


def factor_kernel(grams, inverse):
    rows = lax.broadcasted_iota(jnp.int32, (RANK, RANK), 0)
    cols = lax.broadcasted_iota(jnp.int32, (RANK, RANK), 1)
    gram = sum(part[...] for part in grams)
    work = jnp.concatenate([gram, (rows == cols).astype(F32)], axis=1)
    for start in range(0, RANK, 8):
        column = [jnp.broadcast_to(work[:, start + j : start + j + 1], work.shape) for j in range(8)]
        row = [work[j : j + 1, :] for j in range(8)]
        for j in range(8):
            pivot = column[j][j : j + 1, :]
            inverse[start + j : start + j + 1, :] = (row[j] * lax.rsqrt(pivot))[:, RANK:]
            scaled = row[j] / pivot
            for i in range(j + 1, 8):
                factor = column[i][j : j + 1, :] / pivot
                row[i] = row[i] - column[i][j : j + 1, :] * scaled
                column[i] = column[i] - column[j] * factor
            if start + 8 < RANK:
                work = work - column[j] * scaled
        work = work[8:]


def ready_kernel(core, l_mine, l_other, w_far, factors, w, w_sem):
    load = pltpu.make_async_copy(w_far, w, w_sem)
    load.start()
    for pieces, base in ((l_mine, core[0]), (l_other, 1 - core[0])):
        for start, size in ranges(PART):
            high, low = split(take(pieces, start, size), 2)
            rows = pl.ds(pl.multiple_of(base * OWN + start, 256), size)
            factors[rows, :] = jnp.concatenate([high, high, low], axis=0).T
    load.wait()


def renew_kernel(core, z_mine, z_other, inverse, factors, g, e, w, new_e, new_w, right_out, e_near, w_near, e_sem, w_sem):
    right = right_factor(core, z_mine, z_other, inverse)
    right_out[...] = right
    mixed = product(inverse[...].T, right)
    high, low = split(mixed, 2)
    stack = jnp.concatenate([high, low, high], axis=0)
    stores = []
    for i, (start, size) in enumerate(ranges(LAST)):
        rows = pl.ds(start, size)
        approx = jnp.dot(factors[rows, :], stack, preferred_element_type=F32)
        merged = g[rows, :].astype(F32) + e[rows, :].astype(F32)
        e_near[rows, :] = (merged - approx).astype(BF16)
        stores.append(pltpu.make_async_copy(e_near.at[rows, :], new_e.at[rows, :], e_sem.at[i]))
        stores[-1].start()
        w_near[rows, :] = (w[rows, :].astype(F32) - 0.5 * approx).astype(BF16)
        stores.append(pltpu.make_async_copy(w_near.at[rows, :], new_w.at[rows, :], w_sem.at[i]))
        stores[-1].start()
    for store in stores:
        store.wait()


SCALAR = pl.BlockSpec(memory_space=pltpu.SMEM)
NEAR = pl.BlockSpec(memory_space=pltpu.VMEM)
FAR = pl.BlockSpec(memory_space=pltpu.HBM)
PIECES = jax.ShapeDtypeStruct((TILES, 4, 128), F32)
ZHALF = jax.ShapeDtypeStruct((HALF, COLS), F32)
NEAR_ARRAY = pltpu.VMEM((ROWS, COLS), BF16)
NEAR_HALF = pltpu.VMEM((OWN, COLS), BF16)
SQUARE = jax.ShapeDtypeStruct((RANK, RANK), F32)
STACK = pltpu.VMEM((3 * RANK, COLS), BF16)


def cost(products, nbytes):
    return pl.CostEstimate(flops=2 * ROWS * COLS * RANK * products, bytes_accessed=nbytes, transcendentals=0)


def params(limit):
    return pltpu.CompilerParams(vmem_limit_bytes=limit)


def near(*arrays):
    return [pltpu.with_memory_space_constraint(x, pltpu.VMEM) for x in arrays]


def far(*arrays):
    return [pltpu.with_memory_space_constraint(x, pltpu.HBM) for x in arrays]


def semaphores(count):
    return pltpu.SemaphoreType.DMA((count,))


def first_other_pass(core, q, g, e):
    return pl.pallas_call(
        first_other_kernel,
        in_specs=[SCALAR, FAR, FAR, FAR],
        out_specs=[NEAR] * 5,
        out_shape=[PIECES, pltpu.VMEM((OWN, COLS), F32), NEAR_ARRAY, NEAR_ARRAY, STACK],
        scratch_shapes=[
            pltpu.VMEM((RANK, COLS), F32),
            pltpu.SemaphoreType.DMA,
            semaphores(2 * len(LOAD)),
            semaphores(2 * len(LOAD)),
        ],
        compiler_params=params(LIMIT),
        cost_estimate=cost(3, 4 * ROWS * COLS),
        name="first_other_pass",
    )(core, *far(q, g, e))


def first_own_pass(core, stack, g, e):
    return pl.pallas_call(
        first_own_kernel,
        in_specs=[SCALAR] + [NEAR] * 3,
        out_specs=NEAR,
        out_shape=PIECES,
        compiler_params=params(SMALL),
        cost_estimate=cost(3, 2 * ROWS * COLS),
        name="first_own_pass",
    )(core, *near(stack, g, e))


def first_right_pass(core, left, g, e, received):
    return pl.pallas_call(
        first_right_kernel,
        in_specs=[SCALAR] + [NEAR] * 4,
        out_specs=[NEAR] * 5,
        out_shape=[NEAR_HALF, NEAR_HALF, ZHALF, ZHALF, SQUARE],
        scratch_shapes=[pltpu.VMEM((3 * RANK, OWN), BF16)],
        compiler_params=params(LIMIT),
        cost_estimate=cost(3, 4 * ROWS * COLS),
        name="first_right_pass",
    )(core, left, *near(g, e, received))


def left_pass(core, z_mine, z_other, inverse, high, low):
    return pl.pallas_call(
        left_kernel,
        in_specs=[SCALAR] + [NEAR] * 5,
        out_specs=NEAR,
        out_shape=PIECES,
        scratch_shapes=[STACK],
        compiler_params=params(SMALL),
        cost_estimate=cost(3, 2 * ROWS * COLS),
        name="left_pass",
    )(core, z_mine, z_other, inverse, *near(high, low))


def right_pass(core, left, high, low):
    return pl.pallas_call(
        right_kernel,
        in_specs=[SCALAR] + [NEAR] * 3,
        out_specs=[NEAR] * 3,
        out_shape=[ZHALF, ZHALF, SQUARE],
        scratch_shapes=[pltpu.VMEM((3 * RANK, OWN), BF16)],
        compiler_params=params(SMALL),
        cost_estimate=cost(3, 2 * ROWS * COLS),
        name="right_pass",
    )(core, left, *near(high, low))


def factor(*grams):
    return pl.pallas_call(
        factor_kernel,
        out_shape=SQUARE,
        compiler_params=params(SMALL),
        cost_estimate=pl.CostEstimate(flops=4 * 10**9, bytes_accessed=8 * RANK**2, transcendentals=RANK),
        name="factor",
    )(grams)


def ready(core, l_mine, l_other, w):
    return pl.pallas_call(
        ready_kernel,
        in_specs=[SCALAR, NEAR, NEAR, FAR],
        out_specs=[NEAR] * 2,
        out_shape=[pltpu.VMEM((ROWS, 3 * RANK), BF16), NEAR_ARRAY],
        scratch_shapes=[pltpu.SemaphoreType.DMA],
        compiler_params=params(SMALL),
        cost_estimate=cost(1, 4 * ROWS * COLS),
        name="ready",
    )(core, l_mine, l_other, *far(w))


def renew(core, z_mine, z_other, inverse, factors, g, e, w):
    array = jax.ShapeDtypeStruct((ROWS, COLS), BF16)
    return pl.pallas_call(
        renew_kernel,
        in_specs=[SCALAR] + [NEAR] * 7,
        out_specs=[FAR, FAR, NEAR],
        out_shape=[array, array, jax.ShapeDtypeStruct((RANK, COLS), F32)],
        scratch_shapes=[
            pltpu.VMEM((ROWS, COLS), BF16),
            pltpu.VMEM((ROWS, COLS), BF16),
            semaphores(len(LAST)),
            semaphores(len(LAST)),
        ],
        compiler_params=params(LIMIT),
        cost_estimate=cost(3, 10 * ROWS * COLS),
        name="renew",
    )(core, z_mine, z_other, inverse, *near(factors, g, e, w))


def swap(x):
    return lax.ppermute(x, "core", [(0, 1), (1, 0)])


def along_y(x, shift):
    return lax.ppermute(x, "y", [(i, (i + shift) % 4) for i in range(4)])


def mean(terms):
    return pl.pallas_call(
        mean_kernel,
        out_shape=PIECES,
        compiler_params=params(SMALL),
        cost_estimate=pl.CostEstimate(flops=HALF * ROWS, bytes_accessed=8 * HALF * ROWS, transcendentals=0),
        name="mean",
    )(terms)


def exchange(x):
    x = x.reshape(CHIPS, TILES // CHIPS, 4, 128)
    return lax.all_to_all(x, CHIP_AXES, 0, 0, tiled=True).reshape(TILES, 4, 128)


def mean_left(term):
    return exchange(mean(exchange(term)))


def sum_right(mine, other, gram, run=None):
    half, grams, given = lax.optimization_barrier((mine + swap(other), (gram, swap(gram)), run[1] if run else ()))
    parts = [along_y(half, shift) for shift in (1, 3, 2)]
    parts, inverse, done = lax.optimization_barrier((parts, factor(*grams), run[0](*given) if run else ()))
    half = (half + parts[2]) + (parts[0] + parts[1])
    return (half, swap(half), inverse), done


def shards(gradients, errors, weight, start_q):
    core = lax.axis_index("core").astype(jnp.int32).reshape(1)
    other, send, g, e, stack = first_other_pass(core, start_q.T, gradients[0], errors[0])
    term, send = lax.optimization_barrier((first_own_pass(core, stack, g, e) + swap(other), send))
    left, received = lax.optimization_barrier((mean_left(term), swap(send)))
    high, low, *terms = first_right_pass(core, left, g, e, received)
    right, _ = sum_right(*terms)
    left = mean_left(left_pass(core, *right, high, low))
    left_other = swap(left)
    right, (factors, w) = sum_right(*right_pass(core, left, high, low), (ready, (core, left, left_other, weight)))
    new_e, new_w, right_factor = renew(core, *right, factors, g, e, w)
    return new_e[None], new_w, right_factor.T


def solution(mesh):
    chips = Mesh(mesh.devices.reshape(4, 2, 4, 4), ("y", "core", "x", "z"))
    dp, tensor = ("y", "core"), ("x", "z")
    return jax.shard_map(
        shards,
        mesh=chips,
        in_specs=(P(dp, None, tensor), P(dp, None, tensor), P(None, tensor), P(tensor, None)),
        out_specs=(P(dp, None, tensor), P(None, tensor), P(tensor, None)),
        check_vma=False,
    )
```

```python
import jax
import jax.numpy as jnp
from jax import lax
from jax.experimental import pallas as pl
from jax.experimental.pallas import tpu as pltpu
from jax.sharding import Mesh, PartitionSpec as P

F32, BF16 = jnp.float32, jnp.bfloat16
RANK, HALF = 64, 32
ROWS, COLS = 3072, 768
WIDE = 256
OWN = ROWS // 2
LOAD = (768,) * 2
PART = (512,) * 3
LAST = (256,) * 12
CHIPS = 64
TILES = HALF * ROWS // 512
REPLICAS = 8
CHIP_AXES = ("y", "x", "z")
LIMIT, SMALL = 16 * 2**20, 6 * 2**20


def split(x, parts):
    terms = []
    for _ in range(parts):
        term = x.astype(BF16)
        terms.append(term)
        x = x - term.astype(F32)
    return terms


def fold(x):
    return x[:RANK] + (x[RANK : 2 * RANK] + x[2 * RANK :])


def ordered(core, mine, other):
    first = core == 0
    return jnp.concatenate([jnp.where(first, mine, other), jnp.where(first, other, mine)], axis=0)


def parted(core, x):
    first = core == 0
    top, bottom = x[:HALF], x[HALF:]
    return jnp.where(first, top, bottom), jnp.where(first, bottom, top)


def put(pieces, start, x):
    groups = x.shape[0] // 4
    for lane in range(x.shape[1] // 128):
        for group in range(groups):
            tile = (start // 128 + lane) * groups + group
            pieces[tile] = x[4 * group : 4 * group + 4, 128 * lane : 128 * lane + 128]


def take(pieces, start, size):
    groups = RANK // 4
    columns = []
    for lane in range(start // 128, (start + size) // 128):
        tiles = [pieces[lane * groups + group] for group in range(groups)]
        columns.append(jnp.concatenate(tiles, axis=0))
    return jnp.concatenate(columns, axis=1)


def ranges(sizes):
    starts = [sum(sizes[:i]) for i in range(len(sizes))]
    return list(zip(starts, sizes))


def mean_kernel(terms, out):
    share = terms[...].reshape(CHIPS, TILES // CHIPS, 4, 128)
    total = jnp.sum(share, axis=0) * (1.0 / REPLICAS)
    out[...] = jnp.broadcast_to(total[None], share.shape).reshape(out.shape)


def stacked(x):
    return jnp.concatenate(split(x, 3), axis=0)


def times_rows(stack, g, e, start, size):
    rows = pl.ds(start, size)
    across = (((1,), (1,)), ((), ()))
    p = lax.dot_general(stack[...], g[rows, :], across, preferred_element_type=F32)
    return fold(p + lax.dot_general(stack[...], e[rows, :], across, preferred_element_type=F32))


def first_other_kernel(core, q_far, g_far, e_far, term, send, g, e, stack, q, q_sem, g_sem, e_sem):
    q_copy = pltpu.make_async_copy(q_far, q, q_sem)
    q_copy.start()
    pieces = ranges(LOAD)
    copies = []
    for half in (1 - core[0], core[0]):
        for start, size in pieces:
            rows = pl.ds(pl.multiple_of(half * OWN + start, 256), size)
            slot = len(copies)
            copies.append(
                (
                    pltpu.make_async_copy(g_far.at[rows, :], g.at[rows, :], g_sem.at[slot]),
                    pltpu.make_async_copy(e_far.at[rows, :], e.at[rows, :], e_sem.at[slot]),
                )
            )
    for pair in copies[: len(pieces)]:
        for copy in pair:
            copy.start()
    q_copy.wait()
    stack[...] = stacked(q[...])
    for pair, later in zip(copies, copies[len(pieces) :]):
        for copy in pair:
            copy.wait()
        for copy in later:
            copy.start()
    for start, size in pieces:
        put(term, start, times_rows(stack, g, e, pl.multiple_of((1 - core[0]) * OWN + start, 256), size))
    for start in range(0, OWN, 256):
        rows = pl.ds(pl.multiple_of((1 - core[0]) * OWN + start, 256), 256)
        send[pl.ds(start, 256), :] = g[rows, :].astype(F32) + e[rows, :].astype(F32)
    for pair in copies[len(pieces) :]:
        for copy in pair:
            copy.wait()


def first_own_kernel(core, stack, g, e, term):
    for half in range(2):

        @pl.when(core[0] == half)
        def _():
            for start, size in ranges(PART):
                put(term, start, times_rows(stack, g, e, half * OWN + start, size))


def right_factor(core, z_mine, z_other, inverse):
    z = ordered(core[0], z_mine[...], z_other[...])
    return product(inverse[...], z) * (1.0 / REPLICAS)


def merge_rows(core, g, e, received, high, low, cols):
    for start in range(0, OWN, 256):
        rows = pl.ds(pl.multiple_of(core[0] * OWN + start, 256), 256)
        here = pl.ds(start, 256)
        total = g[rows, cols].astype(F32) + e[rows, cols].astype(F32) + received[here, cols]
        high[here, cols], low[here, cols] = split(total, 2)


def product(a, b):
    left, right = split(a, 3), split(b, 3)
    pairs = ((0, 2), (1, 1), (2, 0), (0, 1), (1, 0), (0, 0))
    left = jnp.concatenate([left[i] for i, _ in pairs], axis=1)
    right = jnp.concatenate([right[j] for _, j in pairs], axis=0)
    return jnp.dot(left, right, preferred_element_type=F32)


def left_kernel(core, z_mine, z_other, inverse, high, low, term, stack):
    stack[...] = stacked(right_factor(core, z_mine, z_other, inverse))
    for start, size in ranges(PART):
        put(term, start, times_rows(stack, high, low, start, size))


def times_columns(core, stack, first, second, z_mine, z_other, cols):
    z = jnp.dot(stack[...], first[:, cols], preferred_element_type=F32)
    z = fold(z + jnp.dot(stack[...], second[:, cols], preferred_element_type=F32))
    z_mine[:, cols], z_other[:, cols] = parted(core[0], z)


def stack_left(left, stack):
    for start, size in ranges(PART):
        stack[:, pl.ds(start, size)] = stacked(take(left, start, size))


def gram_kernel(stack, gram):
    products = lax.dot_general(stack[...], stack[...], (((1,), (1,)), ((), ())), preferred_element_type=F32)
    rows = fold(products)
    gram[...] = rows[:, :RANK] + (rows[:, RANK : 2 * RANK] + rows[:, 2 * RANK :])


def first_right_kernel(core, left, g, e, received, high, low, z_mine, z_other, stack):
    stack_left(left, stack)
    for part in range(COLS // WIDE):
        cols = pl.ds(part * WIDE, WIDE)
        merge_rows(core, g, e, received, high, low, cols)
        times_columns(core, stack, high, low, z_mine, z_other, cols)


def right_kernel(core, left, high, low, z_mine, z_other, stack):
    stack_left(left, stack)
    for part in range(COLS // WIDE):
        times_columns(core, stack, high, low, z_mine, z_other, pl.ds(part * WIDE, WIDE))


def factor_kernel(grams, inverse):
    rows = lax.broadcasted_iota(jnp.int32, (RANK, RANK), 0)
    cols = lax.broadcasted_iota(jnp.int32, (RANK, RANK), 1)
    gram = sum(part[...] for part in grams)
    work = jnp.concatenate([gram, (rows == cols).astype(F32)], axis=1)
    for start in range(0, RANK, 8):
        column = [jnp.broadcast_to(work[:, start + j : start + j + 1], work.shape) for j in range(8)]
        row = [work[j : j + 1, :] for j in range(8)]
        for j in range(8):
            pivot = column[j][j : j + 1, :]
            inverse[start + j : start + j + 1, :] = (row[j] * lax.rsqrt(pivot))[:, RANK:]
            scaled = row[j] / pivot
            for i in range(j + 1, 8):
                factor = column[i][j : j + 1, :] / pivot
                row[i] = row[i] - column[i][j : j + 1, :] * scaled
                column[i] = column[i] - column[j] * factor
            if start + 8 < RANK:
                work = work - column[j] * scaled
        work = work[8:]


def ready_kernel(core, l_mine, l_other, w_far, factors, w, w_sem):
    load = pltpu.make_async_copy(w_far, w, w_sem)
    load.start()
    for pieces, base in ((l_mine, core[0]), (l_other, 1 - core[0])):
        for start, size in ranges(PART):
            high, low = split(take(pieces, start, size), 2)
            rows = pl.ds(pl.multiple_of(base * OWN + start, 256), size)
            factors[rows, :] = jnp.concatenate([high, high, low], axis=0).T
    load.wait()


def renew_kernel(core, z_mine, z_other, inverse, factors, g, e, w, new_e, new_w, right_out, e_near, w_near, e_sem, w_sem):
    right = right_factor(core, z_mine, z_other, inverse)
    right_out[...] = right
    mixed = product(inverse[...].T, right)
    high, low = split(mixed, 2)
    stack = jnp.concatenate([high, low, high], axis=0)
    stores = []
    for i, (start, size) in enumerate(ranges(LAST)):
        rows = pl.ds(start, size)
        approx = jnp.dot(factors[rows, :], stack, preferred_element_type=F32)
        merged = g[rows, :].astype(F32) + e[rows, :].astype(F32)
        e_near[rows, :] = (merged - approx).astype(BF16)
        stores.append(pltpu.make_async_copy(e_near.at[rows, :], new_e.at[rows, :], e_sem.at[i]))
        stores[-1].start()
        w_near[rows, :] = (w[rows, :].astype(F32) - 0.5 * approx).astype(BF16)
        stores.append(pltpu.make_async_copy(w_near.at[rows, :], new_w.at[rows, :], w_sem.at[i]))
        stores[-1].start()
    for store in stores:
        store.wait()


SCALAR = pl.BlockSpec(memory_space=pltpu.SMEM)
NEAR = pl.BlockSpec(memory_space=pltpu.VMEM)
FAR = pl.BlockSpec(memory_space=pltpu.HBM)
PIECES = jax.ShapeDtypeStruct((TILES, 4, 128), F32)
ZHALF = jax.ShapeDtypeStruct((HALF, COLS), F32)
NEAR_ARRAY = pltpu.VMEM((ROWS, COLS), BF16)
NEAR_HALF = pltpu.VMEM((OWN, COLS), BF16)
SQUARE = jax.ShapeDtypeStruct((RANK, RANK), F32)
STACK = pltpu.VMEM((3 * RANK, COLS), BF16)


def cost(products, nbytes):
    return pl.CostEstimate(flops=2 * ROWS * COLS * RANK * products, bytes_accessed=nbytes, transcendentals=0)


def params(limit):
    return pltpu.CompilerParams(vmem_limit_bytes=limit)


def near(*arrays):
    return [pltpu.with_memory_space_constraint(x, pltpu.VMEM) for x in arrays]


def far(*arrays):
    return [pltpu.with_memory_space_constraint(x, pltpu.HBM) for x in arrays]


def semaphores(count):
    return pltpu.SemaphoreType.DMA((count,))


def first_other_pass(core, q, g, e):
    return pl.pallas_call(
        first_other_kernel,
        in_specs=[SCALAR, FAR, FAR, FAR],
        out_specs=[NEAR] * 5,
        out_shape=[PIECES, pltpu.VMEM((OWN, COLS), F32), NEAR_ARRAY, NEAR_ARRAY, STACK],
        scratch_shapes=[
            pltpu.VMEM((RANK, COLS), F32),
            pltpu.SemaphoreType.DMA,
            semaphores(2 * len(LOAD)),
            semaphores(2 * len(LOAD)),
        ],
        compiler_params=params(LIMIT),
        cost_estimate=cost(3, 4 * ROWS * COLS),
        name="first_other_pass",
    )(core, *far(q, g, e))


def first_own_pass(core, stack, g, e):
    return pl.pallas_call(
        first_own_kernel,
        in_specs=[SCALAR] + [NEAR] * 3,
        out_specs=NEAR,
        out_shape=PIECES,
        compiler_params=params(SMALL),
        cost_estimate=cost(3, 2 * ROWS * COLS),
        name="first_own_pass",
    )(core, *near(stack, g, e))


def first_right_pass(core, left, g, e, received):
    return pl.pallas_call(
        first_right_kernel,
        in_specs=[SCALAR] + [NEAR] * 4,
        out_specs=[NEAR] * 5,
        out_shape=[NEAR_HALF, NEAR_HALF, ZHALF, ZHALF, pltpu.VMEM((3 * RANK, OWN), BF16)],
        compiler_params=params(LIMIT),
        cost_estimate=cost(3, 4 * ROWS * COLS),
        name="first_right_pass",
    )(core, left, *near(g, e, received))


def left_pass(core, z_mine, z_other, inverse, high, low):
    return pl.pallas_call(
        left_kernel,
        in_specs=[SCALAR] + [NEAR] * 5,
        out_specs=NEAR,
        out_shape=PIECES,
        scratch_shapes=[STACK],
        compiler_params=params(SMALL),
        cost_estimate=cost(3, 2 * ROWS * COLS),
        name="left_pass",
    )(core, z_mine, z_other, inverse, *near(high, low))


def right_pass(core, left, high, low):
    return pl.pallas_call(
        right_kernel,
        in_specs=[SCALAR] + [NEAR] * 3,
        out_specs=[NEAR] * 3,
        out_shape=[ZHALF, ZHALF, pltpu.VMEM((3 * RANK, OWN), BF16)],
        compiler_params=params(SMALL),
        cost_estimate=cost(3, 2 * ROWS * COLS),
        name="right_pass",
    )(core, left, *near(high, low))


def gram_of(stack):
    return pl.pallas_call(
        gram_kernel,
        in_specs=[NEAR],
        out_specs=NEAR,
        out_shape=SQUARE,
        compiler_params=params(SMALL),
        cost_estimate=pl.CostEstimate(flops=2 * 9 * RANK**2 * OWN, bytes_accessed=6 * RANK * OWN, transcendentals=0),
        name="gram",
    )(*near(stack))


def factor(*grams):
    return pl.pallas_call(
        factor_kernel,
        out_shape=SQUARE,
        compiler_params=params(SMALL),
        cost_estimate=pl.CostEstimate(flops=4 * 10**9, bytes_accessed=8 * RANK**2, transcendentals=RANK),
        name="factor",
    )(grams)


def ready(core, l_mine, l_other, w):
    return pl.pallas_call(
        ready_kernel,
        in_specs=[SCALAR, NEAR, NEAR, FAR],
        out_specs=[NEAR] * 2,
        out_shape=[pltpu.VMEM((ROWS, 3 * RANK), BF16), NEAR_ARRAY],
        scratch_shapes=[pltpu.SemaphoreType.DMA],
        compiler_params=params(SMALL),
        cost_estimate=cost(1, 4 * ROWS * COLS),
        name="ready",
    )(core, l_mine, l_other, *far(w))


def renew(core, z_mine, z_other, inverse, factors, g, e, w):
    array = jax.ShapeDtypeStruct((ROWS, COLS), BF16)
    return pl.pallas_call(
        renew_kernel,
        in_specs=[SCALAR] + [NEAR] * 7,
        out_specs=[FAR, FAR, NEAR],
        out_shape=[array, array, jax.ShapeDtypeStruct((RANK, COLS), F32)],
        scratch_shapes=[
            pltpu.VMEM((ROWS, COLS), BF16),
            pltpu.VMEM((ROWS, COLS), BF16),
            semaphores(len(LAST)),
            semaphores(len(LAST)),
        ],
        compiler_params=params(LIMIT),
        cost_estimate=cost(3, 10 * ROWS * COLS),
        name="renew",
    )(core, z_mine, z_other, inverse, *near(factors, g, e, w))


def swap(x):
    return lax.ppermute(x, "core", [(0, 1), (1, 0)])


def along_y(x, shift):
    return lax.ppermute(x, "y", [(i, (i + shift) % 4) for i in range(4)])


def mean(terms):
    return pl.pallas_call(
        mean_kernel,
        out_shape=PIECES,
        compiler_params=params(SMALL),
        cost_estimate=pl.CostEstimate(flops=HALF * ROWS, bytes_accessed=8 * HALF * ROWS, transcendentals=0),
        name="mean",
    )(terms)


def exchange(x):
    x = x.reshape(CHIPS, TILES // CHIPS, 4, 128)
    return lax.all_to_all(x, CHIP_AXES, 0, 0, tiled=True).reshape(TILES, 4, 128)


def mean_left(term):
    return exchange(mean(exchange(term)))


def sum_right(mine, other, stack, run=None):
    gram = gram_of(stack)
    half, given = lax.optimization_barrier((mine + swap(other), run[1] if run else ()))
    parts = [along_y(half, shift) for shift in (1, 3, 2)]
    parts, inverse, done = lax.optimization_barrier((parts, factor(gram, swap(gram)), run[0](*given) if run else ()))
    half = (half + parts[2]) + (parts[0] + parts[1])
    return (half, swap(half), inverse), done


def shards(gradients, errors, weight, start_q):
    core = lax.axis_index("core").astype(jnp.int32).reshape(1)
    other, send, g, e, stack = first_other_pass(core, start_q.T, gradients[0], errors[0])
    term, send = lax.optimization_barrier((first_own_pass(core, stack, g, e) + swap(other), send))
    left, received = lax.optimization_barrier((mean_left(term), swap(send)))
    high, low, *terms = first_right_pass(core, left, g, e, received)
    right, _ = sum_right(*terms)
    left = mean_left(left_pass(core, *right, high, low))
    left_other = swap(left)
    right, (factors, w) = sum_right(*right_pass(core, left, high, low), (ready, (core, left, left_other, weight)))
    new_e, new_w, right_factor = renew(core, *right, factors, g, e, w)
    return new_e[None], new_w, right_factor.T


def solution(mesh):
    chips = Mesh(mesh.devices.reshape(4, 2, 4, 4), ("y", "core", "x", "z"))
    dp, tensor = ("y", "core"), ("x", "z")
    return jax.shard_map(
        shards,
        mesh=chips,
        in_specs=(P(dp, None, tensor), P(dp, None, tensor), P(None, tensor), P(tensor, None)),
        out_specs=(P(dp, None, tensor), P(None, tensor), P(tensor, None)),
        check_vma=False,
    )
```
